768 devices in a mesh: ray: 96 (over z, y), mp: 8 (over x, core).
Axes of the slice: x: 4, y: 8, z: 12, core: 2. Of those that a mesh axis runs over, the one named last changes fastest.
Arguments:
- ray_matrix: bfloat16 [3072, 32, 128, 128], P('ray', 'mp'), as said below
- block_cols: int32 [3072, 32], P('ray', 'mp'), may hold values from 0 to 95, as said below
- iterate: float32 [8, 96, 16, 128], P('mp', 'ray'), may hold values from -6 to 6
- residual: float32 [3072, 16, 128], P('ray'), may hold values from -6 to 6
Outputs:
- iterate_next: float32 [8, 96, 16, 128], P('mp', 'ray')
- residual_next: float32 [3072, 16, 128], P('ray')
The draws below stay inside these ranges and needn't reach their ends.
Inputs may be any that keep to these rules, and one draw needn't show every extreme that they name: `block_cols`: slot k of a ray block belongs to model group k // 4; every model block of every group is named by at least one ray block. `ray_matrix`: all entries are positive path lengths.
All inputs are finite; a program needn't handle non-finite values.
Results may differ from the reference program's by a relative error of at most 0.00045.
Values may be sent and summed in bfloat16 or wider, within the bound.
A program may use at most 32 MiB of HBM per device.

```python
import math
import jax
import jax.numpy as jnp
from jax import lax

BLOCK = 128
RHS = 16
K_DEV = 4
RB_DEV = 32
MB_DEV = 1
GROUPS = 8
MB_GROUP = 96
RAYBLOCKS = 3072
KB = 32
N_RAY = 96


def block_pattern(key):
    key = jax.random.fold_in(key, 101)
    columns = []
    for group_index in range(GROUPS):
        sub_key = jax.random.fold_in(key, group_index)
        first_key, second_key = jax.random.split(sub_key)
        starts = jax.random.permutation(first_key, RAYBLOCKS) % MB_GROUP
        strides = jax.random.randint(second_key, (RAYBLOCKS, K_DEV), 1, 3)
        offsets = jnp.cumsum(strides, axis=1) - strides[:, :1]
        columns.append((starts[:, None] + offsets) % MB_GROUP)
    return jnp.concatenate(columns, axis=1).astype(jnp.int32)


def draw_block_cols(key, part):
    pattern = block_pattern(key)
    return pattern


def draw_ray_matrix(key, part):
    pattern = block_pattern(key)
    key = jax.random.fold_in(key, 13)
    base_key, row_key, col_key = jax.random.split(key, 3)
    full_shape = (RAYBLOCKS, KB, BLOCK, BLOCK)
    base_part = jnp.exp(jax.random.uniform(base_key, full_shape, jnp.float32, math.log(0.2), 0.0))
    ramp_top = 3.0
    row_pos = jnp.arange(RAYBLOCKS, dtype=jnp.float32) / max(RAYBLOCKS - 1, 1)
    row_spread = jnp.exp(jax.random.uniform(row_key, (RAYBLOCKS, BLOCK), jnp.float32, 0.0, math.log(10.0)))
    row_scale = jnp.sqrt(1.0 + (ramp_top - 1.0) * row_pos)[:, None] * row_spread
    col_pos = jnp.arange(MB_GROUP, dtype=jnp.float32) / max(MB_GROUP - 1, 1)
    col_spread = jnp.exp(jax.random.uniform(col_key, (GROUPS, MB_GROUP, BLOCK), jnp.float32, 0.0, math.log(10.0)))
    col_table = (1.0 + (ramp_top - 1.0) * col_pos)[None, :, None] * col_spread
    group_of = jnp.arange(KB, dtype=jnp.int32) // K_DEV
    col_scale = col_table[group_of[None, :], pattern]
    size_scale = 1.0 / (30.0 * math.sqrt(BLOCK * RB_DEV * K_DEV / MB_DEV))
    return (base_part * row_scale[:, None, :, None] * col_scale[:, :, None, :] * size_scale).astype(jnp.bfloat16)


def levels(stream_key, extent, cuts, least, high):
    loudness, own = 1.0, jax.random.fold_in(stream_key, 6)
    for position, parts in cuts:
        draws = jnp.exp(jax.random.uniform(jax.random.fold_in(own, position), (parts,), jnp.float32, least / len(cuts), high / len(cuts)))
        loudness = loudness * jnp.repeat(draws, extent[position] // parts).reshape([-1 if axis == position else 1 for axis in range(len(extent))])
    return loudness


def normal_values(rng, extent, width, most, cuts=(), kind=jnp.bfloat16):
    loudness = levels(rng, extent, cuts, -0.22, 0.18) if cuts else 1.0
    drawn = jax.random.normal(rng, extent, jnp.float32) * width * loudness
    return jnp.minimum(jnp.maximum(drawn, -most), most).astype(kind)


def setup_inputs(seed: int = 0) -> dict:
    key_of = jax.random.split(jax.random.key(seed), 5)
    ray_matrix = draw_ray_matrix(jax.random.fold_in(key_of[4], 71), 0)
    block_cols = draw_block_cols(jax.random.fold_in(key_of[4], 71), 0)
    iterate = normal_values(key_of[2], (GROUPS, MB_GROUP, RHS, BLOCK), 1.0, 6.0, ((0, 8), (1, 96)), jnp.float32)
    residual = normal_values(key_of[3], (RAYBLOCKS, RHS, BLOCK), 1.0, 6.0, ((0, 96),), jnp.float32)
    return {"ray_matrix": ray_matrix, "block_cols": block_cols, "iterate": iterate, "residual": residual}


eps = 1e-6


def reference(ray_matrix, block_cols, iterate, residual):
    group_count = iterate.shape[0]
    group_len = iterate.shape[1]
    rhs_count = iterate.shape[2]
    block_len = iterate.shape[3]
    slot_count = block_cols.shape[1]
    per_group = slot_count // group_count
    group_of = jnp.arange(slot_count, dtype=jnp.int32) // per_group
    targets = (block_cols + group_of[None, :] * group_len).astype(jnp.int32)
    model_blocks = group_count * group_len
    shard_matrix = ray_matrix.reshape(N_RAY, RB_DEV, slot_count, block_len, block_len)
    shard_targets = targets.reshape(N_RAY, RB_DEV, slot_count)
    shard_rows = residual.reshape(N_RAY, RB_DEV, rhs_count, block_len)

    def transpose_add(running, pieces):
        matrix, target_rows, rows_here = pieces
        rows_low = lax.optimization_barrier(rows_here.astype(jnp.bfloat16))
        unit_row = jnp.ones((RB_DEV, 1, block_len), jnp.bfloat16)
        stacked = jnp.concatenate([rows_low, unit_row], axis=1)
        slot_terms = jnp.einsum("rktc,rht->rkhc", matrix.astype(jnp.float32), stacked.astype(jnp.float32))
        added_part = jax.ops.segment_sum(slot_terms.reshape(RB_DEV * slot_count, rhs_count + 1, block_len), target_rows.reshape(-1), num_segments=model_blocks)
        return running + added_part, None

    start_sum = jnp.zeros((model_blocks, rhs_count + 1, block_len), jnp.float32)
    summed, unused = lax.scan(transpose_add, start_sum, (shard_matrix, shard_targets, shard_rows))
    gradient = summed[:, :rhs_count]
    scaled = gradient / summed[:, rhs_count:]
    grad_norm = jnp.sum(gradient * scaled, axis=(0, 2))
    direction_low = lax.optimization_barrier(scaled.astype(jnp.bfloat16))

    def forward(pieces):
        matrix, target_rows = pieces
        picked = direction_low[target_rows].astype(jnp.float32)
        return jnp.einsum("rktc,rkhc->rht", matrix.astype(jnp.float32), picked)

    image = lax.map(forward, (shard_matrix, shard_targets)).reshape(RB_DEV * N_RAY, rhs_count, block_len)
    image_norm = jnp.sum(image * image, axis=(0, 2))
    step_len = grad_norm / (image_norm + eps)
    iterate_next = iterate + step_len[None, None, :, None] * scaled.reshape(group_count, group_len, rhs_count, block_len)
    residual_next = residual - step_len[None, :, None] * image
    return iterate_next, residual_next
```

```python
import functools
import jax
import jax.numpy as jnp
from jax import lax
from jax.experimental import pallas as pl
from jax.experimental.pallas import tpu as pltpu
from jax.sharding import PartitionSpec as P

MESH = pl.DeviceIdType.MESH
F32 = jnp.float32
BF16 = jnp.bfloat16
eps = 1e-06

NY = 8
H_Y = 10
H_Z = 7
CHUNKS = 8


def kernel(nz, nmp, a_hbm, cols_s, cols_v, it_hbm, res_hbm, itn_ref, resn_ref,
           a_v, res_v, it_v, terms, gy, gz, ry, rz, s2y, s2z, ry2, rz2, grad_v, scaled_v,
           dirs, img_f, img_b, ri, img, nsrc, nz_r, ny_r, nmp_r,
           a_sem, res_sem, it_sem,
           sy, sz, vy, vz, sy2, sz2, vy2, vz2, sa1, va1, sa2, va2,
           si, vi, sg, vg, sn1, vn1, sn2, vn2, sn3, vn3):
    ny = NY
    mb = nz * ny
    rb = a_v.shape[0]
    rb_own = rb // nmp
    per = rb // CHUNKS
    me = lax.axis_index("ray")
    mp = lax.axis_index("mp")
    z = me // ny
    y = me % ny
    y_of = [None] + [(y + d) % ny for d in range(1, ny)]
    z_of = [None] + [(z + d) % nz for d in range(1, nz)]
    mp_of = [None] + [(mp + d) % nmp for d in range(1, nmp)]
    y_id = lambda d: (z * ny + y_of[d], mp)
    z_id = lambda d: (z_of[d] * ny + y, mp)
    mp_id = lambda d: (me, mp_of[d])

    barrier = pltpu.get_barrier_semaphore()
    for d in range(1, nz):
        pl.semaphore_signal(barrier, inc=1, device_id=z_id(d), device_id_type=MESH)
    for d in range(1, ny):
        pl.semaphore_signal(barrier, inc=1, device_id=y_id(d), device_id_type=MESH)
    for d in range(1, nmp):
        pl.semaphore_signal(barrier, inc=1, device_id=mp_id(d), device_id_type=MESH)

    res_copy = pltpu.make_async_copy(res_hbm, res_v, res_sem)
    res_copy.start()
    a_copies = []
    for i in range(CHUNKS):
        part = pl.ds(i * per, per)
        copy = pltpu.make_async_copy(a_hbm.at[part], a_v.at[part], a_sem.at[i])
        copy.start()
        a_copies.append(copy)
    it_copy = pltpu.make_async_copy(it_hbm, it_v, it_sem)
    it_copy.start()

    sends = []

    def push(src, dst, send_sem, recv_sem, target):
        copy = pltpu.make_async_remote_copy(
            src_ref=src, dst_ref=dst, send_sem=send_sem, recv_sem=recv_sem,
            device_id=target, device_id_type=MESH)
        copy.start()
        sends.append(copy)
        return copy

    lane = lax.broadcasted_iota(jnp.int32, (rb, 128), 1)
    slots = cols_v.shape[1]

    def one_hot(place):
        parts = [(place(cols_v[:, k:k + 1]) == lane).astype(F32) for k in range(slots)]
        hot = jnp.concatenate(parts, axis=0).T[:mb].astype(BF16)
        return jnp.concatenate([hot, hot, hot], axis=1)

    hot_z = one_hot(lambda c: c)
    hot_y = one_hot(lambda c: (c % ny) * nz + c // ny)

    tiles = rb * slots
    res_copy.wait()
    ones = jnp.ones((16, 128), BF16)
    for i in range(CHUNKS):
        a_copies[i].wait()

        def products(j, carry):
            r = i * per + j
            left = jnp.concatenate([res_v[r].astype(BF16), ones], axis=0)
            right = jnp.concatenate([a_v[r, k] for k in range(slots)], axis=1)
            out = jnp.dot(left, right, preferred_element_type=F32)
            for k in range(slots):
                terms[pl.ds(k * rb + r, 24, stride=tiles), :] = out[:24, k * 128:(k + 1) * 128]
            return carry

        lax.fori_loop(0, per, products, 0, unroll=True)

    def split(h):
        t = terms[pl.ds(h * tiles, tiles), :]
        hi = t.astype(BF16)
        rest = t - hi.astype(F32)
        mid = rest.astype(BF16)
        low = (rest - mid.astype(F32)).astype(BF16)
        return jnp.concatenate([hi, mid, low], axis=0)

    def segment(hot, dst, rows, first):
        for h in range(0, rows, 2):
            n = min(2, rows - h)
            right = jnp.concatenate([split(first + h + i) for i in range(n)], axis=1)
            out = jnp.dot(hot, right, preferred_element_type=F32)
            for i in range(n):
                dst[pl.ds(h + i, mb, stride=rows), :] = out[:, i * 128:(i + 1) * 128]

    segment(hot_z, gz, H_Z, H_Y)
    pl.semaphore_wait(barrier, nz + ny + nmp - 3)
    len_z = ny * H_Z
    len_y = nz * H_Y
    rs_z = [push(gz.at[pl.ds(z_of[d] * len_z, len_z)], rz.at[d - 1], sz.at[d - 1], vz.at[d - 1], z_id(d))
            for d in range(1, nz)]
    segment(hot_y, gy, H_Y, 0)
    rs_y = [push(gy.at[pl.ds(y_of[d] * len_y, len_y)], ry.at[d - 1], sy.at[d - 1], vy.at[d - 1], y_id(d))
            for d in range(1, ny)]

    acc_y = gy[pl.ds(pl.multiple_of(y * len_y, 8), len_y), :]
    for d in range(1, ny):
        rs_y[d - 1].wait_recv()
        acc_y = acc_y + ry[d - 1]
    for i in range(nz):
        s2y[i, 0:H_Y, :] = acc_y[i * H_Y:(i + 1) * H_Y]
    rs_y2 = [push(s2y.at[z_of[d]], ry2.at[d - 1], sy2.at[d - 1], vy2.at[d - 1], z_id(d))
             for d in range(1, nz)]
    acc_z = gz[pl.ds(pl.multiple_of(z * len_z, 8), len_z), :]
    for d in range(1, nz):
        rs_z[d - 1].wait_recv()
        acc_z = acc_z + rz[d - 1]
    for i in range(ny):
        s2z[i, 0:H_Z, :] = acc_z[i * H_Z:(i + 1) * H_Z]
    rs_z2 = [push(s2z.at[y_of[d]], rz2.at[d - 1], sz2.at[d - 1], vz2.at[d - 1], y_id(d))
             for d in range(1, ny)]

    sum_z = s2z[y]
    for d in range(1, ny):
        rs_z2[d - 1].wait_recv()
        sum_z = sum_z + rz2[d - 1]
    sum_y = s2y[z]
    for d in range(1, nz):
        rs_y2[d - 1].wait_recv()
        sum_y = sum_y + ry2[d - 1]
    grad_v[0:H_Y, :] = sum_y[0:H_Y]
    grad_v[H_Y:16, :] = sum_z[0:H_Z - 1]
    gradient = grad_v[...]
    scaled = gradient / sum_z[H_Z - 1:H_Z]
    scaled_v[...] = scaled

    own = y * nz + z
    dirs[own] = scaled.astype(BF16)
    ag1 = [push(dirs.at[own], dirs.at[own], sa1.at[d - 1], va1.at[d - 1], z_id(d)) for d in range(1, nz)]
    for copy in ag1:
        copy.wait_recv()
    row = pl.ds(y * nz, nz)
    ag2 = [push(dirs.at[row], dirs.at[row], sa2.at[d - 1], va2.at[d - 1], y_id(d)) for d in range(1, ny)]
    for copy in ag2:
        copy.wait_recv()

    def image_of(first):
        def one(j, carry):
            r = first + j
            picked = []
            for k in range(slots):
                c = cols_s[r, k]
                picked.append(dirs[(c % ny) * nz + c // ny])
            left = jnp.concatenate(picked, axis=1)
            right = jnp.concatenate([a_v[r, k] for k in range(slots)], axis=1)
            out = lax.dot_general(left, right, (((1,), (1,)), ((), ())), preferred_element_type=F32)
            img_f[r] = out
            img_b[r] = out.astype(BF16)
            return carry

        lax.fori_loop(0, rb_own, one, 0, unroll=True)

    rs_i = []
    for d in range(1, nmp):
        first = mp_of[d] * rb_own
        image_of(first)
        rs_i.append(push(img_b.at[pl.ds(first, rb_own)], ri.at[d - 1], si.at[d - 1], vi.at[d - 1], mp_id(d)))
    mine = pl.ds(mp * rb_own, rb_own)
    image_of(mp * rb_own)
    total = img_f[mine]
    for d in range(1, nmp):
        rs_i[d - 1].wait_recv()
        total = total + ri[d - 1].astype(F32)
    img[mine] = total

    squares = jnp.concatenate(
        [jnp.sum(total * total, axis=0), gradient * scaled, jnp.zeros((96, 128), F32)], axis=0)
    nsrc[0] = jnp.sum(squares.T, axis=0, keepdims=True)
    n1 = [push(nsrc.at[0], nz_r.at[d - 1], sn1.at[d - 1], vn1.at[d - 1], z_id(d)) for d in range(1, nz)]
    ag_i = [push(img.at[mine], img.at[mine], sg.at[d - 1], vg.at[d - 1], mp_id(d)) for d in range(1, nmp)]
    it_copy.wait()
    acc = nsrc[0]
    for d in range(1, nz):
        n1[d - 1].wait_recv()
        acc = acc + nz_r[d - 1]
    nsrc[1] = acc
    n2 = [push(nsrc.at[1], ny_r.at[d - 1], sn2.at[d - 1], vn2.at[d - 1], y_id(d)) for d in range(1, ny)]
    for d in range(1, ny):
        n2[d - 1].wait_recv()
        acc = acc + ny_r[d - 1]
    nmp_r[mp] = acc
    n3 = [push(nmp_r.at[mp], nmp_r.at[mp], sn3.at[d - 1], vn3.at[d - 1], mp_id(d)) for d in range(1, nmp)]
    for copy in ag_i:
        copy.wait_recv()
    for copy in n3:
        copy.wait_recv()
    acc = nmp_r[0]
    for i in range(1, nmp):
        acc = acc + nmp_r[i]
    wide = jnp.broadcast_to(acc, (16, 128))
    sub = lax.broadcasted_iota(jnp.int32, (16, 128), 0)
    lane16 = lax.broadcasted_iota(jnp.int32, (16, 128), 1)
    image_norm = jnp.sum(jnp.where(lane16 == sub, wide, 0.0), axis=1, keepdims=True)
    grad_norm = jnp.sum(jnp.where(lane16 == sub + 16, wide, 0.0), axis=1, keepdims=True)
    step = grad_norm / (image_norm + eps)
    itn_ref[0, 0] = it_v[0, 0] + step * scaled_v[...]
    resn_ref[...] = res_v[...] - step[None] * img[...]
    for copy in sends:
        copy.wait_send()


def local(ray_matrix, block_cols, iterate, residual):
    nmp = lax.axis_size("mp")
    nz = lax.axis_size("ray") // NY
    rb, slots = block_cols.shape
    mb = nz * NY
    rb_own = rb // nmp
    vmem = lambda *shape: pltpu.VMEM(shape, F32)
    dma = lambda n: pltpu.SemaphoreType.DMA((n,))
    scratch = [
        pltpu.VMEM(ray_matrix.shape, BF16),
        pltpu.VMEM(residual.shape, F32),
        pltpu.VMEM(iterate.shape, F32),
        vmem(24 * rb * slots, 128),
        vmem(mb * H_Y, 128),
        vmem(mb * H_Z, 128),
        vmem(NY - 1, nz * H_Y, 128),
        vmem(nz - 1, NY * H_Z, 128),
        vmem(nz, 16, 128),
        vmem(NY, 8, 128),
        vmem(nz - 1, 16, 128),
        vmem(NY - 1, 8, 128),
        vmem(16, 128),
        vmem(16, 128),
        pltpu.VMEM((mb, 16, 128), BF16),
        vmem(rb, 16, 128),
        pltpu.VMEM((rb, 16, 128), BF16),
        pltpu.VMEM((nmp - 1, rb_own, 16, 128), BF16),
        vmem(rb, 16, 128),
        vmem(2, 1, 128),
        vmem(nz - 1, 1, 128),
        vmem(NY - 1, 1, 128),
        vmem(nmp, 1, 128),
        dma(CHUNKS), pltpu.SemaphoreType.DMA, pltpu.SemaphoreType.DMA,
    ]
    y, z, m = NY - 1, nz - 1, nmp - 1
    for n in (y, z, y, z, z, y, z, y, z, z, y, y, m, m, m, m, z, z, y, y, m, m):
        scratch.append(dma(n))
    any_spec = pl.BlockSpec(memory_space=pl.ANY)
    return pl.pallas_call(
        functools.partial(kernel, nz, nmp),
        out_shape=(
            jax.ShapeDtypeStruct(iterate.shape, F32),
            jax.ShapeDtypeStruct(residual.shape, F32),
        ),
        in_specs=[any_spec, pl.BlockSpec(memory_space=pltpu.SMEM), pl.BlockSpec(memory_space=pltpu.VMEM),
                  any_spec, any_spec],
        out_specs=(pl.BlockSpec(memory_space=pltpu.VMEM),) * 2,
        scratch_shapes=scratch,
        compiler_params=pltpu.CompilerParams(
            collective_id=0, has_side_effects=True, vmem_limit_bytes=48 * 2**20),
        cost_estimate=pl.CostEstimate(flops=300_000_000, bytes_accessed=5_000_000, transcendentals=0),
        name="cgls",
    )(ray_matrix, block_cols, block_cols, iterate, residual)


def solution(mesh):
    in_specs = (
        P("ray", "mp", None, None),
        P("ray", "mp"),
        P("mp", "ray", None, None),
        P("ray", None, None),
    )
    out_specs = (P("mp", "ray", None, None), P("ray", None, None))
    return jax.shard_map(local, mesh=mesh, in_specs=in_specs, out_specs=out_specs, check_vma=False)
```

```python
import functools
import jax
import jax.numpy as jnp
from jax import lax
from jax.experimental import pallas as pl
from jax.experimental.pallas import tpu as pltpu
from jax.sharding import PartitionSpec as P

MESH = pl.DeviceIdType.MESH
F32 = jnp.float32
BF16 = jnp.bfloat16
eps = 1e-06

NY = 8
H_Y = 10
H_Z = 7
CHUNKS = 8


def kernel(nz, nmp, a_hbm, cols_hbm, it_hbm, res_hbm, itn_ref, resn_ref,
           a_v, res_v, it_v, cols_v, cols_s, terms, gy, gz, ry, rz, s2y, s2z, ry2, rz2, grad_v, scaled_v,
           dirs, img_f, img_b, ri, img, nsrc, n1_r, n2_r,
           a_sem, res_sem, it_sem, cv_sem, cs_sem,
           sy, sz, vy, vz, sy2, sz2, vy2, vz2, sa1, va1, sa2, va2,
           si, vi, sg, vg, sn1, vn1, sn2, vn2):
    ny = NY
    mb = nz * ny
    rb = a_v.shape[0]
    rb_own = rb // nmp
    per = rb // CHUNKS
    me = lax.axis_index("ray")
    mp = lax.axis_index("mp")
    z = me // ny
    y = me % ny
    y_of = [None] + [(y + d) % ny for d in range(1, ny)]
    z_of = [None] + [(z + d) % nz for d in range(1, nz)]
    mp_of = [None] + [(mp + d) % nmp for d in range(1, nmp)]
    y_id = lambda d: (z * ny + y_of[d], mp)
    z_id = lambda d: (z_of[d] * ny + y, mp)
    mp_id = lambda d: (me, mp_of[d])

    nx = nmp // 2
    x = mp // 2
    core = mp % 2
    other_core = x * 2 + 1 - core

    def zc_id(i):
        if i < nz - 1:
            return z_id(i + 1)
        d = i - (nz - 1)
        return (((z + d) % nz) * ny + y, other_core)

    def yx_id(i):
        return (z * ny + (y + i % ny) % ny, ((x + i // ny) % nx) * 2 + core)

    barrier = pltpu.get_barrier_semaphore()
    for d in range(1, nz):
        pl.semaphore_signal(barrier, inc=1, device_id=z_id(d), device_id_type=MESH)
    for d in range(1, ny):
        pl.semaphore_signal(barrier, inc=1, device_id=y_id(d), device_id_type=MESH)
    for d in range(1, nmp):
        pl.semaphore_signal(barrier, inc=1, device_id=mp_id(d), device_id_type=MESH)
    for i in range(nz, 2 * nz - 1):
        pl.semaphore_signal(barrier, inc=1, device_id=zc_id(i), device_id_type=MESH)
    for i in range(ny, nx * ny):
        if i % ny:
            pl.semaphore_signal(barrier, inc=1, device_id=yx_id(i), device_id_type=MESH)
    greeted = (nz - 1) + (ny - 1) + (nmp - 1) + (nz - 1) + (nx - 1) * (ny - 1)

    cv_copy = pltpu.make_async_copy(cols_hbm, cols_v, cv_sem)
    cv_copy.start()
    res_copy = pltpu.make_async_copy(res_hbm, res_v, res_sem)
    res_copy.start()
    a_copies = []
    for i in range(CHUNKS):
        part = pl.ds(i * per, per)
        copy = pltpu.make_async_copy(a_hbm.at[part], a_v.at[part], a_sem.at[i])
        copy.start()
        a_copies.append(copy)
    it_copy = pltpu.make_async_copy(it_hbm, it_v, it_sem)
    it_copy.start()
    cs_copy = pltpu.make_async_copy(cols_hbm, cols_s, cs_sem)
    cs_copy.start()

    sends = []

    def push(src, dst, send_sem, recv_sem, target):
        copy = pltpu.make_async_remote_copy(
            src_ref=src, dst_ref=dst, send_sem=send_sem, recv_sem=recv_sem,
            device_id=target, device_id_type=MESH)
        copy.start()
        sends.append(copy)
        return copy

    block = lax.broadcasted_iota(jnp.int32, (mb, rb), 0)
    slots = cols_v.shape[0]

    def one_hot(place):
        parts = [(place(cols_v[k:k + 1, :]) == block).astype(F32) for k in range(slots)]
        hot = jnp.concatenate(parts, axis=1).astype(BF16)
        return jnp.concatenate([hot, hot, hot], axis=1)

    cv_copy.wait()
    hot_z = one_hot(lambda c: c)
    hot_y = one_hot(lambda c: (c % ny) * nz + c // ny)

    tiles = rb * slots
    res_copy.wait()
    ones = jnp.ones((16, 128), BF16)
    for i in range(CHUNKS):
        a_copies[i].wait()

        def products(j, carry):
            r = i * per + j
            left = jnp.concatenate([res_v[r].astype(BF16), ones], axis=0)
            right = jnp.concatenate([a_v[r, k] for k in range(slots)], axis=1)
            out = jnp.dot(left, right, preferred_element_type=F32)
            for k in range(slots):
                terms[pl.ds(k * rb + r, 24, stride=tiles), :] = out[:24, k * 128:(k + 1) * 128]
            return carry

        lax.fori_loop(0, per, products, 0, unroll=True)

    def split(h):
        t = terms[pl.ds(h * tiles, tiles), :]
        hi = t.astype(BF16)
        rest = t - hi.astype(F32)
        mid = rest.astype(BF16)
        low = (rest - mid.astype(F32)).astype(BF16)
        return jnp.concatenate([hi, mid, low], axis=0)

    def segment(hot, dst, rows, first):
        for h in range(0, rows, 2):
            n = min(2, rows - h)
            right = jnp.concatenate([split(first + h + i) for i in range(n)], axis=1)
            out = jnp.dot(hot, right, preferred_element_type=F32)
            for i in range(n):
                dst[pl.ds(h + i, mb, stride=rows), :] = out[:, i * 128:(i + 1) * 128]

    segment(hot_z, gz, H_Z, H_Y)
    pl.semaphore_wait(barrier, greeted)
    len_z = ny * H_Z
    len_y = nz * H_Y
    rs_z = [push(gz.at[pl.ds(z_of[d] * len_z, len_z)], rz.at[d - 1], sz.at[d - 1], vz.at[d - 1], z_id(d))
            for d in range(1, nz)]
    segment(hot_y, gy, H_Y, 0)
    rs_y = [push(gy.at[pl.ds(y_of[d] * len_y, len_y)], ry.at[d - 1], sy.at[d - 1], vy.at[d - 1], y_id(d))
            for d in range(1, ny)]

    acc_y = gy[pl.ds(pl.multiple_of(y * len_y, 8), len_y), :]
    for d in range(1, ny):
        rs_y[d - 1].wait_recv()
        acc_y = acc_y + ry[d - 1]
    for i in range(nz):
        s2y[i, 0:H_Y, :] = acc_y[i * H_Y:(i + 1) * H_Y]
    rs_y2 = [push(s2y.at[z_of[d], pl.ds(0, H_Y)], ry2.at[d - 1, pl.ds(0, H_Y)], sy2.at[d - 1], vy2.at[d - 1], z_id(d))
             for d in range(1, nz)]
    acc_z = gz[pl.ds(pl.multiple_of(z * len_z, 8), len_z), :]
    for d in range(1, nz):
        rs_z[d - 1].wait_recv()
        acc_z = acc_z + rz[d - 1]
    for i in range(ny):
        s2z[i, 0:H_Z, :] = acc_z[i * H_Z:(i + 1) * H_Z]
    rs_z2 = [push(s2z.at[y_of[d]], rz2.at[d - 1], sz2.at[d - 1], vz2.at[d - 1], y_id(d))
             for d in range(1, ny)]

    sum_z = s2z[y]
    for d in range(1, ny):
        rs_z2[d - 1].wait_recv()
        sum_z = sum_z + rz2[d - 1]
    sum_y = s2y[z, 0:H_Y]
    for d in range(1, nz):
        rs_y2[d - 1].wait_recv()
        sum_y = sum_y + ry2[d - 1, 0:H_Y]
    grad_v[0:H_Y, :] = sum_y
    grad_v[H_Y:16, :] = sum_z[0:H_Z - 1]
    gradient = grad_v[...]
    scaled = gradient / sum_z[H_Z - 1:H_Z]
    scaled_v[...] = scaled

    own = y * nz + z
    dirs[own] = scaled.astype(BF16)
    ag1 = [push(dirs.at[own], dirs.at[own], sa1.at[d - 1], va1.at[d - 1], z_id(d)) for d in range(1, nz)]
    for copy in ag1:
        copy.wait_recv()
    row = pl.ds(y * nz, nz)
    ag2 = [push(dirs.at[row], dirs.at[row], sa2.at[d - 1], va2.at[d - 1], y_id(d)) for d in range(1, ny)]
    for copy in ag2:
        copy.wait_recv()

    cs_copy.wait()

    def image_of(first):
        def one(j, carry):
            r = first + j
            picked = []
            for k in range(slots):
                c = cols_s[k, r]
                picked.append(dirs[(c % ny) * nz + c // ny])
            left = jnp.concatenate(picked, axis=1)
            right = jnp.concatenate([a_v[r, k] for k in range(slots)], axis=1)
            out = lax.dot_general(left, right, (((1,), (1,)), ((), ())), preferred_element_type=F32)
            img_f[r] = out
            img_b[r] = out.astype(BF16)
            return carry

        lax.fori_loop(0, rb_own, one, 0, unroll=True)

    rs_i = []
    for d in range(1, nmp):
        first = mp_of[d] * rb_own
        image_of(first)
        rs_i.append(push(img_b.at[pl.ds(first, rb_own)], ri.at[d - 1], si.at[d - 1], vi.at[d - 1], mp_id(d)))
    mine = pl.ds(mp * rb_own, rb_own)
    image_of(mp * rb_own)
    total = img_f[mine]
    for d in range(1, nmp):
        rs_i[d - 1].wait_recv()
        total = total + ri[d - 1].astype(F32)
    img[mine] = total

    squares = jnp.concatenate(
        [jnp.sum(total * total, axis=0), gradient * scaled, jnp.zeros((96, 128), F32)], axis=0)
    nsrc[0] = jnp.sum(squares.T, axis=0, keepdims=True)
    n1 = [push(nsrc.at[0], n1_r.at[i], sn1.at[i], vn1.at[i], zc_id(i)) for i in range(2 * nz - 1)]
    ag_i = [push(img.at[mine], img.at[mine], sg.at[d - 1], vg.at[d - 1], mp_id(d)) for d in range(1, nmp)]
    it_copy.wait()
    for copy in n1:
        copy.wait_recv()
    acc = nsrc[0]
    for i in range(nz - 1):
        acc = acc + n1_r[i]
    other = n1_r[nz - 1]
    for i in range(nz, 2 * nz - 1):
        other = other + n1_r[i]
    own_x = pl.ds(x * ny, 1)
    n2_r[own_x] = (acc + other)[None]
    n2 = [push(n2_r.at[own_x], n2_r.at[pl.ds(x * ny + i % ny, 1)], sn2.at[i - 1], vn2.at[i - 1], yx_id(i))
          for i in range(1, nx * ny)]
    for copy in ag_i:
        copy.wait_recv()
    for copy in n2:
        copy.wait_recv()
    acc = n2_r[0]
    for i in range(1, nx * ny):
        acc = acc + n2_r[i]
    wide = jnp.broadcast_to(acc, (16, 128))
    sub = lax.broadcasted_iota(jnp.int32, (16, 128), 0)
    lane16 = lax.broadcasted_iota(jnp.int32, (16, 128), 1)
    image_norm = jnp.sum(jnp.where(lane16 == sub, wide, 0.0), axis=1, keepdims=True)
    grad_norm = jnp.sum(jnp.where(lane16 == sub + 16, wide, 0.0), axis=1, keepdims=True)
    step = grad_norm / (image_norm + eps)
    itn_ref[0, 0] = it_v[0, 0] + step * scaled_v[...]
    resn_ref[...] = res_v[...] - step[None] * img[...]
    for copy in sends:
        copy.wait_send()


def local(ray_matrix, block_cols, iterate, residual):
    nmp = lax.axis_size("mp")
    nz = lax.axis_size("ray") // NY
    rb, slots = block_cols.shape
    mb = nz * NY
    rb_own = rb // nmp
    vmem = lambda *shape: pltpu.VMEM(shape, F32)
    dma = lambda n: pltpu.SemaphoreType.DMA((n,))
    scratch = [
        pltpu.VMEM(ray_matrix.shape, BF16),
        pltpu.VMEM(residual.shape, F32),
        pltpu.VMEM(iterate.shape, F32),
        pltpu.VMEM((slots, rb), jnp.int32),
        pltpu.SMEM((slots, rb), jnp.int32),
        vmem(24 * rb * slots, 128),
        vmem(mb * H_Y, 128),
        vmem(mb * H_Z, 128),
        vmem(NY - 1, nz * H_Y, 128),
        vmem(nz - 1, NY * H_Z, 128),
        vmem(nz, 16, 128),
        vmem(NY, 8, 128),
        vmem(nz - 1, 16, 128),
        vmem(NY - 1, 8, 128),
        vmem(16, 128),
        vmem(16, 128),
        pltpu.VMEM((mb, 16, 128), BF16),
        vmem(rb, 16, 128),
        pltpu.VMEM((rb, 16, 128), BF16),
        pltpu.VMEM((nmp - 1, rb_own, 16, 128), BF16),
        vmem(rb, 16, 128),
        vmem(1, 1, 128),
        vmem(2 * nz - 1, 1, 128),
        vmem(nmp // 2 * NY, 1, 128),
        dma(CHUNKS), *[pltpu.SemaphoreType.DMA] * 4,
    ]
    y, z, m = NY - 1, nz - 1, nmp - 1
    zc, yx = 2 * nz - 1, nmp // 2 * NY - 1
    for n in (y, z, y, z, z, y, z, y, z, z, y, y, m, m, m, m, zc, zc, yx, yx):
        scratch.append(dma(n))
    any_spec = pl.BlockSpec(memory_space=pl.ANY)
    return pl.pallas_call(
        functools.partial(kernel, nz, nmp),
        out_shape=(
            jax.ShapeDtypeStruct(iterate.shape, F32),
            jax.ShapeDtypeStruct(residual.shape, F32),
        ),
        in_specs=[any_spec] * 4,
        out_specs=(pl.BlockSpec(memory_space=pltpu.VMEM),) * 2,
        scratch_shapes=scratch,
        compiler_params=pltpu.CompilerParams(
            collective_id=0, has_side_effects=True, vmem_limit_bytes=61 * 2**20),
        cost_estimate=pl.CostEstimate(flops=300_000_000, bytes_accessed=5_000_000, transcendentals=0),
        name="cgls",
    )(ray_matrix, block_cols.T, iterate, residual)


def solution(mesh):
    in_specs = (
        P("ray", "mp", None, None),
        P("ray", "mp"),
        P("mp", "ray", None, None),
        P("ray", None, None),
    )
    out_specs = (P("mp", "ray", None, None), P("ray", None, None))
    return jax.shard_map(local, mesh=mesh, in_specs=in_specs, out_specs=out_specs, check_vma=False)
```

```python
import functools
import jax
import jax.numpy as jnp
from jax import lax
from jax.experimental import pallas as pl
from jax.experimental.pallas import tpu as pltpu
from jax.sharding import PartitionSpec as P

MESH = pl.DeviceIdType.MESH
F32 = jnp.float32
BF16 = jnp.bfloat16
eps = 1e-06

NY = 8
H_Y = 10
H_Z = 7
CHUNKS = 8
GROUPS = 3


def far_first(n):
    return sorted(range(1, n), key=lambda d: -min(d, n - d))


def place_of(rel, n):
    return n - 1 - 2 * rel if rel < n // 2 else 2 * rel - n


def kernel(nz, nmp, a_hbm, cols_hbm, res_hbm, small_ref, img_hbm,
           a_v, res_v, cols_v, place_v, place_s, terms, gy, gz, ry, rz, s2y, s2z, ry2, rz2, grad_v,
           dirs, img_f, img_b, ri, img, nsrc, n1_r, n2_r,
           a_sem, res_sem, cv_sem, ps_sem, out_sem,
           sy, sz, vy, vz, sy2, sz2, vy2, vz2, sa1, va1, sa2, va2,
           si, vi, sg, vg, sn1, vn1, sn2, vn2):
    ny = NY
    mb = nz * ny
    rb = a_v.shape[0]
    rb_own = rb // nmp
    per = rb // CHUNKS
    me = lax.axis_index("ray")
    mp = lax.axis_index("mp")
    z = me // ny
    y = me % ny
    y_of = [None] + [(y + d) % ny for d in range(1, ny)]
    z_of = [None] + [(z + d) % nz for d in range(1, nz)]
    mp_of = [None] + [(mp + d) % nmp for d in range(1, nmp)]
    y_id = lambda d: (z * ny + y_of[d], mp)
    z_id = lambda d: (z_of[d] * ny + y, mp)
    mp_id = lambda d: (me, mp_of[d])

    nx = nmp // 2
    x = mp // 2
    core = mp % 2
    other_core = x * 2 + 1 - core

    def zc_id(i):
        if i < nz - 1:
            return z_id(i + 1)
        d = i - (nz - 1)
        return (((z + d) % nz) * ny + y, other_core)

    def yx_id(i):
        return (z * ny + (y + i % ny) % ny, ((x + i // ny) % nx) * 2 + core)

    barrier = pltpu.get_barrier_semaphore()
    for d in far_first(nz):
        pl.semaphore_signal(barrier, inc=1, device_id=z_id(d), device_id_type=MESH)
    for d in far_first(ny):
        pl.semaphore_signal(barrier, inc=1, device_id=y_id(d), device_id_type=MESH)
    for d in range(1, nmp):
        pl.semaphore_signal(barrier, inc=1, device_id=mp_id(d), device_id_type=MESH)
    for i in range(nz, 2 * nz - 1):
        pl.semaphore_signal(barrier, inc=1, device_id=zc_id(i), device_id_type=MESH)
    for i in range(ny, nx * ny):
        if i % ny:
            pl.semaphore_signal(barrier, inc=1, device_id=yx_id(i), device_id_type=MESH)
    greeted = (nz - 1) + (ny - 1) + (nmp - 1) + (nz - 1) + (nx - 1) * (ny - 1)

    cv_copy = pltpu.make_async_copy(cols_hbm, cols_v, cv_sem)
    cv_copy.start()
    res_copy = pltpu.make_async_copy(res_hbm, res_v, res_sem)
    res_copy.start()
    a_copies = []
    for i in range(CHUNKS):
        part = pl.ds(i * per, per)
        copy = pltpu.make_async_copy(a_hbm.at[part], a_v.at[part], a_sem.at[i])
        copy.start()
        a_copies.append(copy)

    sends = []

    def push(src, dst, send_sem, recv_sem, target):
        copy = pltpu.make_async_remote_copy(
            src_ref=src, dst_ref=dst, send_sem=send_sem, recv_sem=recv_sem,
            device_id=target, device_id_type=MESH)
        copy.start()
        sends.append(copy)
        return copy

    block = lax.broadcasted_iota(jnp.int32, (mb, rb), 0)
    slots = cols_v.shape[0]

    def one_hot(place):
        parts = [(place(cols_v[k:k + 1, :]) == block).astype(F32) for k in range(slots)]
        hot = jnp.concatenate(parts, axis=1).astype(BF16)
        return jnp.concatenate([hot, hot, hot], axis=1)

    cv_copy.wait()

    def near(c, mine, n):
        rel = c - mine
        rel = jnp.where(rel < 0, rel + n, rel)
        return jnp.where(rel < n // 2, n - 1 - 2 * rel, 2 * rel - n)

    place_z = lambda c: (c // ny) * ny + near(c % ny, y, ny)
    place_y = lambda c: (c % ny) * nz + near(c // ny, z, nz)
    hot_z = one_hot(place_z)
    hot_y = one_hot(place_y)
    place_v[...] = place_y(cols_v[...])
    place_copy = pltpu.make_async_copy(place_v, place_s, ps_sem)
    place_copy.start()

    tiles = rb * slots
    res_copy.wait()
    ones = jnp.ones((16, 128), BF16)
    for i in range(CHUNKS):
        a_copies[i].wait()

        def products(j, carry):
            r = i * per + j
            left = jnp.concatenate([res_v[r].astype(BF16), ones], axis=0)
            right = jnp.concatenate([a_v[r, k] for k in range(slots)], axis=1)
            out = jnp.dot(left, right, preferred_element_type=F32)
            for k in range(slots):
                terms[pl.ds(k * rb + r, 24, stride=tiles), :] = out[:24, k * 128:(k + 1) * 128]
            return carry

        lax.fori_loop(0, per, products, 0, unroll=True)

    def split(h):
        t = terms[pl.ds(h * tiles, tiles), :]
        hi = t.astype(BF16)
        rest = t - hi.astype(F32)
        mid = rest.astype(BF16)
        low = (rest - mid.astype(F32)).astype(BF16)
        return jnp.concatenate([hi, mid, low], axis=0)

    def segment(hot, dst, rows, first):
        for h in range(0, rows, 2):
            n = min(2, rows - h)
            right = jnp.concatenate([split(first + h + i) for i in range(n)], axis=1)
            out = jnp.dot(hot, right, preferred_element_type=F32)
            for i in range(n):
                dst[pl.ds(h + i, mb, stride=rows), :] = out[:, i * 128:(i + 1) * 128]

    segment(hot_z, gz, H_Z, H_Y)
    pl.semaphore_wait(barrier, greeted)
    len_z = ny * H_Z
    len_y = nz * H_Y
    rs_z = {d: push(gz.at[pl.ds(z_of[d] * len_z, len_z)], rz.at[d - 1], sz.at[d - 1], vz.at[d - 1], z_id(d))
            for d in far_first(nz)}
    segment(hot_y, gy, H_Y, 0)
    len_g = len_y // GROUPS
    places_g = nz // GROUPS
    rs_y = {}
    for g in range(GROUPS):
        for d in far_first(ny):
            i = (d - 1) * GROUPS + g
            rs_y[d, g] = push(gy.at[pl.ds(y_of[d] * len_y + g * len_g, len_g)],
                              ry.at[d - 1, pl.ds(g * len_g, len_g)], sy.at[i], vy.at[i], y_id(d))
    rel_of = {place_of(rel, nz): rel for rel in range(nz)}
    rs_y2 = {}

    def sum_group(g):
        part = gy[pl.ds(pl.multiple_of(y * len_y + g * len_g, 8), len_g), :]
        for d in far_first(ny):
            rs_y[d, g].wait_recv()
        for d in range(1, ny):
            part = part + ry[d - 1, g * len_g:(g + 1) * len_g]
        for i in range(places_g):
            place = g * places_g + i
            s2y[place, 0:H_Y, :] = part[i * H_Y:(i + 1) * H_Y]
            d = rel_of[place]
            if d:
                rs_y2[d] = push(s2y.at[place, pl.ds(0, H_Y)], ry2.at[d - 1, pl.ds(0, H_Y)],
                                sy2.at[d - 1], vy2.at[d - 1], z_id(d))

    for g in range(GROUPS - 1):
        sum_group(g)
    acc_z = gz[pl.ds(pl.multiple_of(z * len_z, 8), len_z), :]
    for d in far_first(nz):
        rs_z[d].wait_recv()
    for d in range(1, nz):
        acc_z = acc_z + rz[d - 1]
    for i in range(ny):
        s2z[i, 0:H_Z, :] = acc_z[i * H_Z:(i + 1) * H_Z]
    rs_z2 = {d: push(s2z.at[place_of(d, ny)], rz2.at[d - 1], sz2.at[d - 1], vz2.at[d - 1], y_id(d))
             for d in far_first(ny)}
    sum_group(GROUPS - 1)

    sum_z = s2z[ny - 1]
    for d in range(1, ny):
        rs_z2[d].wait_recv()
        sum_z = sum_z + rz2[d - 1]
    sum_y = s2y[nz - 1, 0:H_Y]
    for d in range(1, nz):
        rs_y2[d].wait_recv()
        sum_y = sum_y + ry2[d - 1, 0:H_Y]
    grad_v[0:H_Y, :] = sum_y
    grad_v[H_Y:16, :] = sum_z[0:H_Z - 1]
    gradient = grad_v[...]
    scaled = gradient / sum_z[H_Z - 1:H_Z]

    first_own = y * nz
    own = first_own + nz - 1
    dirs[own] = scaled.astype(BF16)
    ag1 = {d: push(dirs.at[own], dirs.at[first_own + place_of(nz - d, nz)], sa1.at[d - 1], va1.at[d - 1], z_id(d))
           for d in far_first(nz)}
    ag2 = []
    for g in reversed(range(GROUPS)):
        for place in range(g * places_g, (g + 1) * places_g):
            if rel_of[place]:
                ag1[nz - rel_of[place]].wait_recv()
        part = pl.ds(first_own + g * places_g, places_g)
        for d in far_first(ny):
            i = (d - 1) * GROUPS + g
            ag2.append(push(dirs.at[part], dirs.at[part], sa2.at[i], va2.at[i], y_id(d)))
    place_copy.wait()
    for copy in ag2:
        copy.wait_recv()

    def image_of(first):
        def one(j, carry):
            r = first + j
            picked = []
            for k in range(slots):
                picked.append(dirs[place_s[k, r]])
            left = jnp.concatenate(picked, axis=1)
            right = jnp.concatenate([a_v[r, k] for k in range(slots)], axis=1)
            out = lax.dot_general(left, right, (((1,), (1,)), ((), ())), preferred_element_type=F32)
            img_f[r] = out
            img_b[r] = out.astype(BF16)
            return carry

        lax.fori_loop(0, rb_own, one, 0, unroll=True)

    rs_i = []
    for d in range(1, nmp):
        first = mp_of[d] * rb_own
        image_of(first)
        rs_i.append(push(img_b.at[pl.ds(first, rb_own)], ri.at[d - 1], si.at[d - 1], vi.at[d - 1], mp_id(d)))
    mine = pl.ds(mp * rb_own, rb_own)
    image_of(mp * rb_own)
    total = img_f[mine]
    for d in range(1, nmp):
        rs_i[d - 1].wait_recv()
        total = total + ri[d - 1].astype(F32)
    img[mine] = total

    squares = jnp.concatenate(
        [jnp.sum(total * total, axis=0), gradient * scaled, jnp.zeros((96, 128), F32)], axis=0)
    nsrc[0] = jnp.sum(squares.T, axis=0, keepdims=True)
    n1 = [push(nsrc.at[0], n1_r.at[i], sn1.at[i], vn1.at[i], zc_id(i)) for i in range(2 * nz - 1)]
    ag_i = [push(img.at[mine], img.at[mine], sg.at[d - 1], vg.at[d - 1], mp_id(d)) for d in range(1, nmp)]
    for copy in n1:
        copy.wait_recv()
    acc = nsrc[0]
    for i in range(nz - 1):
        acc = acc + n1_r[i]
    other = n1_r[nz - 1]
    for i in range(nz, 2 * nz - 1):
        other = other + n1_r[i]
    own_x = pl.ds(x * ny, 1)
    n2_r[own_x] = (acc + other)[None]
    n2 = [push(n2_r.at[own_x], n2_r.at[pl.ds(x * ny + i % ny, 1)], sn2.at[i - 1], vn2.at[i - 1], yx_id(i))
          for i in range(1, nx * ny)]
    for copy in ag_i:
        copy.wait_recv()
    out_copy = pltpu.make_async_copy(img, img_hbm, out_sem)
    out_copy.start()
    for copy in n2:
        copy.wait_recv()
    acc = n2_r[0]
    for i in range(1, nx * ny):
        acc = acc + n2_r[i]
    wide = jnp.broadcast_to(acc, (16, 128))
    sub = lax.broadcasted_iota(jnp.int32, (16, 128), 0)
    lane16 = lax.broadcasted_iota(jnp.int32, (16, 128), 1)
    image_norm = jnp.sum(jnp.where(lane16 == sub, wide, 0.0), axis=1, keepdims=True)
    grad_norm = jnp.sum(jnp.where(lane16 == sub + 16, wide, 0.0), axis=1, keepdims=True)
    step = grad_norm / (image_norm + eps)
    small_ref[0] = scaled
    small_ref[1] = jnp.broadcast_to(step, (16, 128))
    out_copy.wait()
    for copy in sends:
        copy.wait_send()


def update(small_ref, img_ref, it_ref, res_ref, itn_ref, resn_ref):
    step = small_ref[1]
    itn_ref[0, 0] = it_ref[0, 0] + step * small_ref[0]
    resn_ref[...] = res_ref[...] - step[None] * img_ref[...]


def local(ray_matrix, block_cols, iterate, residual):
    nmp = lax.axis_size("mp")
    nz = lax.axis_size("ray") // NY
    rb, slots = block_cols.shape
    mb = nz * NY
    rb_own = rb // nmp
    vmem = lambda *shape: pltpu.VMEM(shape, F32)
    dma = lambda n: pltpu.SemaphoreType.DMA((n,))
    scratch = [
        pltpu.VMEM(ray_matrix.shape, BF16),
        pltpu.VMEM(residual.shape, F32),
        pltpu.VMEM((slots, rb), jnp.int32),
        pltpu.VMEM((slots, rb), jnp.int32),
        pltpu.SMEM((slots, rb), jnp.int32),
        vmem(24 * rb * slots, 128),
        vmem(mb * H_Y, 128),
        vmem(mb * H_Z, 128),
        vmem(NY - 1, nz * H_Y, 128),
        vmem(nz - 1, NY * H_Z, 128),
        vmem(nz, 16, 128),
        vmem(NY, 8, 128),
        vmem(nz - 1, 16, 128),
        vmem(NY - 1, 8, 128),
        vmem(16, 128),
        pltpu.VMEM((mb, 16, 128), BF16),
        vmem(rb, 16, 128),
        pltpu.VMEM((rb, 16, 128), BF16),
        pltpu.VMEM((nmp - 1, rb_own, 16, 128), BF16),
        vmem(rb, 16, 128),
        vmem(1, 1, 128),
        vmem(2 * nz - 1, 1, 128),
        vmem(nmp // 2 * NY, 1, 128),
        dma(CHUNKS), *[pltpu.SemaphoreType.DMA] * 4,
    ]
    y, z, m = NY - 1, nz - 1, nmp - 1
    zc, yx = 2 * nz - 1, nmp // 2 * NY - 1
    yg = y * GROUPS
    for n in (yg, z, yg, z, z, y, z, y, z, z, yg, yg, m, m, m, m, zc, zc, yx, yx):
        scratch.append(dma(n))
    any_spec = pl.BlockSpec(memory_space=pl.ANY)
    small, img = pl.pallas_call(
        functools.partial(kernel, nz, nmp),
        out_shape=(
            jax.ShapeDtypeStruct((2, 16, 128), F32),
            jax.ShapeDtypeStruct(residual.shape, F32),
        ),
        in_specs=[any_spec] * 3,
        out_specs=(pl.BlockSpec(memory_space=pltpu.VMEM), any_spec),
        scratch_shapes=scratch,
        compiler_params=pltpu.CompilerParams(
            collective_id=0, has_side_effects=True, vmem_limit_bytes=61 * 2**20),
        cost_estimate=pl.CostEstimate(flops=300_000_000, bytes_accessed=5_000_000, transcendentals=0),
        name="cgls",
    )(ray_matrix, block_cols.T, residual)
    return pl.pallas_call(
        update,
        out_shape=(
            jax.ShapeDtypeStruct(iterate.shape, F32),
            jax.ShapeDtypeStruct(residual.shape, F32),
        ),
        in_specs=[pl.BlockSpec(memory_space=pltpu.VMEM)] * 4,
        out_specs=(pl.BlockSpec(memory_space=pltpu.VMEM),) * 2,
        compiler_params=pltpu.CompilerParams(vmem_limit_bytes=61 * 2**20),
        cost_estimate=pl.CostEstimate(flops=200_000, bytes_accessed=800_000, transcendentals=0),
        name="update",
    )(small, img, iterate, residual)


def solution(mesh):
    in_specs = (
        P("ray", "mp", None, None),
        P("ray", "mp"),
        P("mp", "ray", None, None),
        P("ray", None, None),
    )
    out_specs = (P("mp", "ray", None, None), P("ray", None, None))
    return jax.shard_map(local, mesh=mesh, in_specs=in_specs, out_specs=out_specs, check_vma=False)
```

```python
import functools
import jax
import jax.numpy as jnp
from jax import lax
from jax.experimental import pallas as pl
from jax.experimental.pallas import tpu as pltpu
from jax.sharding import PartitionSpec as P

MESH = pl.DeviceIdType.MESH
F32 = jnp.float32
BF16 = jnp.bfloat16
eps = 1e-06

NY = 8
H_Y = 11
H_Z = 6
PAD = 16
CHUNKS = 8
RS_CUTS = (0, 8)
AG_CUTS = (0, 3, 7)

RS_Z, RS_Y, RS_Z2, RS_Y2, AG_1, AG_2, RS_I, AG_I, N_1, N_2, PHASES = 0, 1, 3, 4, 5, 8, 9, 10, 11, 12, 13


def far_first(n):
    return sorted(range(1, n), key=lambda d: -min(d, n - d))


def place_of(rel, n):
    return n - 1 - 2 * rel if rel < n // 2 else 2 * rel - n


def kernel(nz, nmp, a_hbm, cols_hbm, res_hbm, small_ref, img_hbm,
           a_v, res_v, cols_v, place_v, place_s, terms, gy, gz, ry, rz, s2y, s2z, ry2, rz2, grad_v,
           dirs, img_f, img_b, ri, img, nsrc, n1_r, n2_r,
           a_sem, res_sem, cv_sem, ps_sem, out_sem,
           send_sem, recv_sem):
    ny = NY
    mb = nz * ny
    rb = a_v.shape[0]
    rb_own = rb // nmp
    per = rb // CHUNKS
    me = lax.axis_index("ray")
    mp = lax.axis_index("mp")
    z = me // ny
    y = me % ny
    y_of = [None] + [(y + d) % ny for d in range(1, ny)]
    z_of = [None] + [(z + d) % nz for d in range(1, nz)]
    y_id = lambda d: (z * ny + y_of[d], mp)
    z_id = lambda d: (z_of[d] * ny + y, mp)

    nx = nmp // 2
    x = mp // 2
    core = mp % 2
    other_core = x * 2 + 1 - core
    mp_of = [((x + d) % nx) * 2 + c for d in far_first(nx) for c in (core, 1 - core)] + [other_core]
    mp_id = lambda i: (me, mp_of[i])

    def zc_id(i):
        if i < nz - 1:
            return z_id(i + 1)
        d = i - (nz - 1)
        return (((z + d) % nz) * ny + y, other_core)

    def yx_id(i):
        return (z * ny + (y + i % ny) % ny, ((x + i // ny) % nx) * 2 + core)

    cv_copy = pltpu.make_async_copy(cols_hbm, cols_v, cv_sem)
    cv_copy.start()
    res_copy = pltpu.make_async_copy(res_hbm, res_v, res_sem)
    res_copy.start()
    a_copies = []
    for i in range(CHUNKS):
        part = pl.ds(i * per, per)
        copy = pltpu.make_async_copy(a_hbm.at[part], a_v.at[part], a_sem.at[i])
        copy.start()
        a_copies.append(copy)

    barrier = pltpu.get_barrier_semaphore()
    for d in far_first(nz):
        pl.semaphore_signal(barrier, inc=1, device_id=z_id(d), device_id_type=MESH)
    for d in far_first(ny):
        pl.semaphore_signal(barrier, inc=1, device_id=y_id(d), device_id_type=MESH)
    for d in range(nmp - 1):
        pl.semaphore_signal(barrier, inc=1, device_id=mp_id(d), device_id_type=MESH)
    for i in range(nz, 2 * nz - 1):
        pl.semaphore_signal(barrier, inc=1, device_id=zc_id(i), device_id_type=MESH)
    for i in range(ny, nx * ny):
        if i % ny:
            pl.semaphore_signal(barrier, inc=1, device_id=yx_id(i), device_id_type=MESH)
    greeted = (nz - 1) + (ny - 1) + (nmp - 1) + (nz - 1) + (nx - 1) * (ny - 1)

    def push(src, dst, phase, target, group=0):
        pltpu.make_async_remote_copy(
            src_ref=src, dst_ref=dst, send_sem=send_sem.at[phase], recv_sem=recv_sem.at[phase + group],
            device_id=target, device_id_type=MESH).start()

    def all_of(ref, phase, group=0):
        return pltpu.make_async_remote_copy(
            src_ref=ref, dst_ref=ref, send_sem=send_sem.at[phase], recv_sem=recv_sem.at[phase + group],
            device_id=y_id(1), device_id_type=MESH)

    def received(ref, phase, group=0):
        all_of(ref, phase, group).wait_recv()

    def sent(ref, phase):
        all_of(ref, phase).wait_send()

    slots = cols_v.shape[0]

    def one_hot(blocks, place):
        block = lax.broadcasted_iota(jnp.int32, (blocks, rb), 0)
        parts = [(place(cols_v[k:k + 1, :]) == block).astype(F32) for k in range(slots)]
        hot = jnp.concatenate(parts, axis=1).astype(BF16)
        return jnp.concatenate([hot, hot, hot], axis=1)

    cv_copy.wait()

    def near(c, mine, n):
        rel = c - mine
        rel = jnp.where(rel < 0, rel + n, rel)
        return jnp.where(rel < n // 2, n - 1 - 2 * rel, 2 * rel - n)

    near_z = lambda c: near(c // ny, z, nz)
    hot_z = one_hot(mb, lambda c: (c // ny) * ny + near(c % ny, y, ny))
    hot_y = one_hot(ny * PAD, lambda c: (c % ny) * PAD + near_z(c))
    place_v[...] = (cols_v[...] % ny) * nz + near_z(cols_v[...])
    place_copy = pltpu.make_async_copy(place_v, place_s, ps_sem)
    place_copy.start()

    tiles = rb * slots
    res_copy.wait()
    ones = jnp.ones((16, 128), BF16)
    for i in range(CHUNKS):
        a_copies[i].wait()

        def products(j, carry):
            r = i * per + j
            left = jnp.concatenate([res_v[r].astype(BF16), ones], axis=0)
            right = jnp.concatenate([a_v[r, k] for k in range(slots)], axis=1)
            out = jnp.dot(left, right, preferred_element_type=F32)
            for k in range(slots):
                terms[pl.ds(k * rb + r, 24, stride=tiles), :] = out[:24, k * 128:(k + 1) * 128]
            return carry

        lax.fori_loop(0, per, products, 0, unroll=True)

    def split(h):
        t = terms[pl.ds(h * tiles, tiles), :]
        hi = t.astype(BF16)
        rest = t - hi.astype(F32)
        mid = rest.astype(BF16)
        low = (rest - mid.astype(F32)).astype(BF16)
        return jnp.concatenate([hi, mid, low], axis=0)

    def segment(hot, dst, rows, first):
        for h in range(0, rows, 2):
            n = min(2, rows - h)
            right = jnp.concatenate([split(first + h + i) for i in range(n)], axis=1)
            out = jnp.dot(hot, right, preferred_element_type=F32)
            for i in range(n):
                dst[pl.ds(h + i, hot.shape[0], stride=rows), :] = out[:, i * 128:(i + 1) * 128]

    segment(hot_z, gz, H_Z, H_Y)
    pl.semaphore_wait(barrier, greeted)
    len_z = ny * H_Z
    len_y = PAD * H_Y
    for d in far_first(nz):
        push(gz.at[pl.ds(z_of[d] * len_z, len_z)], rz.at[d - 1], RS_Z, z_id(d))
    segment(hot_y, gy, H_Y, 0)
    groups = list(zip(RS_CUTS, RS_CUTS[1:] + (nz,)))
    rows_of = lambda low, high: pl.ds(low * H_Y, -(-(high - low) * H_Y // 8) * 8)
    for g, (low, high) in enumerate(groups):
        rows = rows_of(low, high)
        for d in far_first(ny):
            push(gy.at[pl.ds(y_of[d] * len_y + rows.start, rows.size)], ry.at[d - 1, rows], RS_Y, y_id(d), g)
    rel_of = {place_of(rel, nz): rel for rel in range(nz)}

    def sum_group(g):
        low, high = groups[g]
        rows = rows_of(low, high)
        part = gy[pl.ds(pl.multiple_of(y * len_y + rows.start, 8), rows.size), :]
        received(ry.at[:, rows], RS_Y, g)
        for d in range(1, ny):
            part = part + ry[d - 1, rows]
        for i in range(high - low):
            place = low + i
            s2y[place, 0:H_Y, :] = part[i * H_Y:(i + 1) * H_Y]
            d = rel_of[place]
            if d:
                push(s2y.at[place, pl.ds(0, H_Y)], ry2.at[d - 1, pl.ds(0, H_Y)], RS_Y2, z_id(d))

    for g in range(len(groups) - 1):
        sum_group(g)
    acc_z = gz[pl.ds(pl.multiple_of(z * len_z, 8), len_z), :]
    received(rz, RS_Z)
    for d in range(1, nz):
        acc_z = acc_z + rz[d - 1]
    for i in range(ny):
        s2z[i, 0:H_Z, :] = acc_z[i * H_Z:(i + 1) * H_Z]
    for d in far_first(ny):
        push(s2z.at[place_of(d, ny)], rz2.at[d - 1], RS_Z2, y_id(d))
    sum_group(len(groups) - 1)

    sum_z = s2z[ny - 1]
    received(rz2, RS_Z2)
    for d in range(1, ny):
        sum_z = sum_z + rz2[d - 1]
    sum_y = s2y[nz - 1, 0:H_Y]
    received(ry2.at[:, pl.ds(0, H_Y)], RS_Y2)
    for d in range(1, nz):
        sum_y = sum_y + ry2[d - 1, 0:H_Y]
    grad_v[0:H_Y, :] = sum_y
    grad_v[H_Y:16, :] = sum_z[0:H_Z - 1]
    gradient = grad_v[...]
    scaled = gradient / sum_z[H_Z - 1:H_Z]

    first_own = y * nz
    own = first_own + nz - 1
    dirs[own] = scaled.astype(BF16)
    cuts = list(zip(AG_CUTS, AG_CUTS[1:] + (nz,)))
    for d in far_first(nz):
        place = place_of(nz - d, nz)
        group = max(g for g, (low, high) in enumerate(cuts) if low <= place)
        push(dirs.at[own], dirs.at[first_own + place], AG_1, z_id(d), group)
    sent(rz, RS_Z)
    sent(ry.at[:, pl.ds(0, sum(rows_of(low, high).size for low, high in groups))], RS_Y)
    sent(rz2, RS_Z2)
    sent(ry2.at[:, pl.ds(0, H_Y)], RS_Y2)
    for g, (low, high) in reversed(list(enumerate(cuts))):
        received(dirs.at[pl.ds(first_own + low, min(high, nz - 1) - low)], AG_1, g)
        part = pl.ds(first_own + low, high - low)
        for d in far_first(ny):
            push(dirs.at[part], dirs.at[part], AG_2, y_id(d))
    place_copy.wait()
    sent(dirs.at[pl.ds(0, nz - 1)], AG_1)
    received(dirs.at[pl.ds(0, mb - nz)], AG_2)

    def image_of(first):
        def one(j, carry):
            r = first + j
            picked = []
            for k in range(slots):
                picked.append(dirs[place_s[k, r]])
            left = jnp.concatenate(picked, axis=1)
            right = jnp.concatenate([a_v[r, k] for k in range(slots)], axis=1)
            out = lax.dot_general(left, right, (((1,), (1,)), ((), ())), preferred_element_type=F32)
            img_f[r] = out
            img_b[r] = out.astype(BF16)
            return carry

        lax.fori_loop(0, rb_own, one, 0, unroll=True)

    for i in range(nmp - 1):
        first = mp_of[i] * rb_own
        image_of(first)
        push(img_b.at[pl.ds(first, rb_own)], ri.at[i], RS_I, mp_id(i))
    mine = pl.ds(mp * rb_own, rb_own)
    image_of(mp * rb_own)
    total = img_f[mine]
    received(ri, RS_I)
    for i in range(nmp - 1):
        total = total + ri[i].astype(F32)
    img[mine] = total

    squares = jnp.concatenate(
        [jnp.sum(total * total, axis=0), gradient * scaled, jnp.zeros((96, 128), F32)], axis=0)
    nsrc[0] = jnp.sum(squares.T, axis=0, keepdims=True)
    for i in range(2 * nz - 1):
        push(nsrc.at[0], n1_r.at[i], N_1, zc_id(i))
    for i in range(nmp - 1):
        push(img.at[mine], img.at[mine], AG_I, mp_id(i))
    sent(dirs.at[pl.ds(0, mb - nz)], AG_2)
    sent(ri, RS_I)
    received(n1_r, N_1)
    acc = nsrc[0]
    for i in range(nz - 1):
        acc = acc + n1_r[i]
    other = n1_r[nz - 1]
    for i in range(nz, 2 * nz - 1):
        other = other + n1_r[i]
    own_x = pl.ds(x * ny, 1)
    n2_r[own_x] = (acc + other)[None]
    for i in range(1, nx * ny):
        push(n2_r.at[own_x], n2_r.at[pl.ds(x * ny + i % ny, 1)], N_2, yx_id(i))
    sent(n1_r, N_1)
    received(img.at[pl.ds(0, rb - rb_own)], AG_I)
    out_copy = pltpu.make_async_copy(img, img_hbm, out_sem)
    out_copy.start()
    sent(img.at[pl.ds(0, rb - rb_own)], AG_I)
    received(n2_r.at[pl.ds(0, nx * ny - 1)], N_2)
    acc = n2_r[0]
    for i in range(1, nx * ny):
        acc = acc + n2_r[i]
    wide = jnp.broadcast_to(acc, (16, 128))
    sub = lax.broadcasted_iota(jnp.int32, (16, 128), 0)
    lane16 = lax.broadcasted_iota(jnp.int32, (16, 128), 1)
    image_norm = jnp.sum(jnp.where(lane16 == sub, wide, 0.0), axis=1, keepdims=True)
    grad_norm = jnp.sum(jnp.where(lane16 == sub + 16, wide, 0.0), axis=1, keepdims=True)
    step = grad_norm / (image_norm + eps)
    small_ref[0] = scaled
    small_ref[1] = jnp.broadcast_to(step, (16, 128))
    out_copy.wait()
    sent(n2_r.at[pl.ds(0, nx * ny - 1)], N_2)


def update(small_ref, img_ref, it_ref, res_ref, itn_ref, resn_ref):
    step = small_ref[1]
    itn_ref[0, 0] = it_ref[0, 0] + step * small_ref[0]
    resn_ref[...] = res_ref[...] - step[None] * img_ref[...]


def local(ray_matrix, block_cols, iterate, residual):
    nmp = lax.axis_size("mp")
    nz = lax.axis_size("ray") // NY
    rb, slots = block_cols.shape
    mb = nz * NY
    rb_own = rb // nmp
    vmem = lambda *shape: pltpu.VMEM(shape, F32)
    dma = lambda n: pltpu.SemaphoreType.DMA((n,))
    scratch = [
        pltpu.VMEM(ray_matrix.shape, BF16),
        pltpu.VMEM(residual.shape, F32),
        pltpu.VMEM((slots, rb), jnp.int32),
        pltpu.VMEM((slots, rb), jnp.int32),
        pltpu.SMEM((slots, rb), jnp.int32),
        vmem(24 * rb * slots, 128),
        vmem(NY * PAD * H_Y, 128),
        vmem(mb * H_Z, 128),
        vmem(NY - 1, PAD * H_Y, 128),
        vmem(nz - 1, NY * H_Z, 128),
        vmem(nz, 16, 128),
        vmem(NY, 8, 128),
        vmem(nz - 1, 16, 128),
        vmem(NY - 1, 8, 128),
        vmem(16, 128),
        pltpu.VMEM((mb, 16, 128), BF16),
        vmem(rb, 16, 128),
        pltpu.VMEM((rb, 16, 128), BF16),
        pltpu.VMEM((nmp - 1, rb_own, 16, 128), BF16),
        vmem(rb, 16, 128),
        vmem(1, 1, 128),
        vmem(2 * nz - 1, 1, 128),
        vmem(nmp // 2 * NY, 1, 128),
        dma(CHUNKS), *[pltpu.SemaphoreType.DMA] * 4,
    ]
    scratch += [dma(PHASES), dma(PHASES)]
    any_spec = pl.BlockSpec(memory_space=pl.ANY)
    small, img = pl.pallas_call(
        functools.partial(kernel, nz, nmp),
        out_shape=(
            jax.ShapeDtypeStruct((2, 16, 128), F32),
            jax.ShapeDtypeStruct(residual.shape, F32),
        ),
        in_specs=[any_spec] * 3,
        out_specs=(pl.BlockSpec(memory_space=pltpu.VMEM), any_spec),
        scratch_shapes=scratch,
        compiler_params=pltpu.CompilerParams(
            collective_id=0, has_side_effects=True, vmem_limit_bytes=61 * 2**20),
        cost_estimate=pl.CostEstimate(flops=300_000_000, bytes_accessed=5_000_000, transcendentals=0),
        name="cgls",
    )(ray_matrix, block_cols.T, residual)
    return pl.pallas_call(
        update,
        out_shape=(
            jax.ShapeDtypeStruct(iterate.shape, F32),
            jax.ShapeDtypeStruct(residual.shape, F32),
        ),
        in_specs=[pl.BlockSpec(memory_space=pltpu.VMEM)] * 4,
        out_specs=(pl.BlockSpec(memory_space=pltpu.VMEM),) * 2,
        compiler_params=pltpu.CompilerParams(vmem_limit_bytes=61 * 2**20),
        cost_estimate=pl.CostEstimate(flops=200_000, bytes_accessed=800_000, transcendentals=0),
        name="update",
    )(small, img, iterate, residual)


def solution(mesh):
    in_specs = (
        P("ray", "mp", None, None),
        P("ray", "mp"),
        P("mp", "ray", None, None),
        P("ray", None, None),
    )
    out_specs = (P("mp", "ray", None, None), P("ray", None, None))
    return jax.shard_map(local, mesh=mesh, in_specs=in_specs, out_specs=out_specs, check_vma=False)
```

```python
import functools
import jax
import jax.numpy as jnp
from jax import lax
from jax.experimental import pallas as pl
from jax.experimental.pallas import tpu as pltpu
from jax.sharding import PartitionSpec as P

MESH = pl.DeviceIdType.MESH
F32 = jnp.float32
BF16 = jnp.bfloat16
eps = 1e-06

NY = 8
H_Y = 11
H_Z = 6
CHUNKS = 8
RS_CUTS = (0, 4, 9)
STRIDE = 8
RZ_CUTS = (0, 4)
AG_CUTS = (0, 3, 7)

RS_Z, RS_Y, RS_Z2, RS_Y2, AG_1, AG_2, RS_I, AG_I, N_1, N_2, PHASES = 0, 2, 5, 6, 7, 10, 11, 12, 13, 14, 15
PAD = STRIDE * len(RS_CUTS)


def far_first(n):
    return sorted(range(1, n), key=lambda d: -min(d, n - d))


def place_of(rel, n):
    return n - 1 - 2 * rel if rel < n // 2 else 2 * rel - n


def kernel(nz, nmp, a_hbm, cols_hbm, res_hbm, small_ref, img_hbm,
           a_v, res_v, cols_v, place_v, place_s, terms, gy, gz, ry, rz, s2y, s2z, ry2, rz2, grad_v,
           dirs, img_f, img_b, ri, img, nsrc, n1_r, n2_r,
           a_sem, res_sem, cv_sem, ps_sem, out_sem,
           send_sem, recv_sem):
    ny = NY
    mb = nz * ny
    rb = a_v.shape[0]
    rb_own = rb // nmp
    per = rb // CHUNKS
    me = lax.axis_index("ray")
    mp = lax.axis_index("mp")
    z = me // ny
    y = me % ny
    y_of = [None] + [(y + d) % ny for d in range(1, ny)]
    z_of = [None] + [(z + d) % nz for d in range(1, nz)]
    y_id = lambda d: (z * ny + y_of[d], mp)
    z_id = lambda d: (z_of[d] * ny + y, mp)

    nx = nmp // 2
    x = mp // 2
    core = mp % 2
    other_core = x * 2 + 1 - core
    mp_of = [((x + d) % nx) * 2 + c for d in far_first(nx) for c in (core, 1 - core)] + [other_core]
    mp_id = lambda i: (me, mp_of[i])

    def zc_id(i):
        if i < nz - 1:
            return z_id(i + 1)
        d = i - (nz - 1)
        return (((z + d) % nz) * ny + y, other_core)

    def yx_id(i):
        return (z * ny + (y + i % ny) % ny, ((x + i // ny) % nx) * 2 + core)

    cv_copy = pltpu.make_async_copy(cols_hbm, cols_v, cv_sem)
    cv_copy.start()
    res_copy = pltpu.make_async_copy(res_hbm, res_v, res_sem)
    res_copy.start()
    a_copies = []
    for i in range(CHUNKS):
        part = pl.ds(i * per, per)
        copy = pltpu.make_async_copy(a_hbm.at[part], a_v.at[part], a_sem.at[i])
        copy.start()
        a_copies.append(copy)

    barrier = pltpu.get_barrier_semaphore()
    for d in far_first(nz):
        pl.semaphore_signal(barrier, inc=1, device_id=z_id(d), device_id_type=MESH)
    for d in far_first(ny):
        pl.semaphore_signal(barrier, inc=1, device_id=y_id(d), device_id_type=MESH)
    for d in range(nmp - 1):
        pl.semaphore_signal(barrier, inc=1, device_id=mp_id(d), device_id_type=MESH)
    for i in range(nz, 2 * nz - 1):
        pl.semaphore_signal(barrier, inc=1, device_id=zc_id(i), device_id_type=MESH)
    for i in range(ny, nx * ny):
        if i % ny:
            pl.semaphore_signal(barrier, inc=1, device_id=yx_id(i), device_id_type=MESH)
    greeted = (nz - 1) + (ny - 1) + (nmp - 1) + (nz - 1) + (nx - 1) * (ny - 1)

    def push(src, dst, phase, target, group=0):
        pltpu.make_async_remote_copy(
            src_ref=src, dst_ref=dst, send_sem=send_sem.at[phase], recv_sem=recv_sem.at[phase + group],
            device_id=target, device_id_type=MESH).start()

    def all_of(ref, phase, group=0):
        return pltpu.make_async_remote_copy(
            src_ref=ref, dst_ref=ref, send_sem=send_sem.at[phase], recv_sem=recv_sem.at[phase + group],
            device_id=y_id(1), device_id_type=MESH)

    def received(ref, phase, group=0):
        all_of(ref, phase, group).wait_recv()

    def sent(ref, phase):
        all_of(ref, phase).wait_send()

    slots = cols_v.shape[0]

    def one_hot(blocks, place):
        block = lax.broadcasted_iota(jnp.int32, (blocks, rb), 0)
        parts = [(place(cols_v[k:k + 1, :]) == block).astype(F32) for k in range(slots)]
        hot = jnp.concatenate(parts, axis=1).astype(BF16)
        return jnp.concatenate([hot, hot, hot], axis=1)

    cv_copy.wait()

    def near(c, mine, n):
        rel = c - mine
        rel = jnp.where(rel < 0, rel + n, rel)
        return jnp.where(rel < n // 2, n - 1 - 2 * rel, 2 * rel - n)

    near_z = lambda c: near(c // ny, z, nz)

    def spot(place):
        return place + sum(
            jnp.where(place >= low, STRIDE - low + last, 0) for last, low in zip(RS_CUTS, RS_CUTS[1:]))

    hot_z = one_hot(mb, lambda c: (c // ny) * ny + near(c % ny, y, ny))
    hot_y = one_hot(ny * PAD, lambda c: (c % ny) * PAD + spot(near_z(c)))
    place_v[...] = (cols_v[...] % ny) * nz + near_z(cols_v[...])
    place_copy = pltpu.make_async_copy(place_v, place_s, ps_sem)
    place_copy.start()

    tiles = rb * slots
    res_copy.wait()
    ones = jnp.ones((16, 128), BF16)
    for i in range(CHUNKS):
        a_copies[i].wait()

        def products(j, carry):
            r = i * per + j
            left = jnp.concatenate([res_v[r].astype(BF16), ones], axis=0)
            right = jnp.concatenate([a_v[r, k] for k in range(slots)], axis=1)
            out = jnp.dot(left, right, preferred_element_type=F32)
            for k in range(slots):
                terms[pl.ds(k * rb + r, 24, stride=tiles), :] = out[:24, k * 128:(k + 1) * 128]
            return carry

        lax.fori_loop(0, per, products, 0, unroll=True)

    def split(h):
        t = terms[pl.ds(h * tiles, tiles), :]
        hi = t.astype(BF16)
        rest = t - hi.astype(F32)
        mid = rest.astype(BF16)
        low = (rest - mid.astype(F32)).astype(BF16)
        return jnp.concatenate([hi, mid, low], axis=0)

    def segment(hot, dst, rows, first):
        for h in range(0, rows, 2):
            n = min(2, rows - h)
            right = jnp.concatenate([split(first + h + i) for i in range(n)], axis=1)
            out = jnp.dot(hot, right, preferred_element_type=F32)
            for i in range(n):
                dst[pl.ds(h + i, hot.shape[0], stride=rows), :] = out[:, i * 128:(i + 1) * 128]

    segment(hot_y, gy, H_Y, 0)
    pl.semaphore_wait(barrier, greeted)
    len_z = ny * H_Z
    len_y = PAD * H_Y
    groups = list(zip(RS_CUTS, RS_CUTS[1:] + (nz,)))
    rows_of = lambda g: pl.ds(g * STRIDE * H_Y, (groups[g][1] - groups[g][0]) * H_Y)
    groups_z = list(zip(RZ_CUTS, RZ_CUTS[1:] + (ny,)))
    rows_z = lambda g: pl.ds(groups_z[g][0] * H_Z, (groups_z[g][1] - groups_z[g][0]) * H_Z)
    for g in range(len(groups)):
        rows = rows_of(g)
        for d in far_first(ny):
            push(gy.at[pl.ds(y_of[d] * len_y + rows.start, rows.size)], ry.at[d - 1, rows], RS_Y, y_id(d), g)
    segment(hot_z, gz, H_Z, H_Y)
    for g in range(len(groups_z)):
        rows = rows_z(g)
        for d in far_first(nz):
            push(gz.at[pl.ds(z_of[d] * len_z + rows.start, rows.size)], rz.at[d - 1, rows], RS_Z, z_id(d), g)
    rel_of = {place_of(rel, nz): rel for rel in range(nz)}

    def sum_group(g):
        low, high = groups[g]
        rows = rows_of(g)
        part = gy[pl.ds(pl.multiple_of(y * len_y + rows.start, 8), rows.size), :]
        received(ry.at[:, rows], RS_Y, g)
        for d in range(1, ny):
            part = part + ry[d - 1, rows]
        for i in range(high - low):
            place = low + i
            s2y[place, 0:H_Y, :] = part[i * H_Y:(i + 1) * H_Y]
            d = rel_of[place]
            if d:
                push(s2y.at[place, pl.ds(0, H_Y)], ry2.at[d - 1, pl.ds(0, H_Y)], RS_Y2, z_id(d))

    rel_z = {place_of(rel, ny): rel for rel in range(ny)}

    def sum_group_z(g):
        low, high = groups_z[g]
        rows = rows_z(g)
        part = gz[pl.ds(pl.multiple_of(z * len_z + rows.start, 8), rows.size), :]
        received(rz.at[:, rows], RS_Z, g)
        for d in range(1, nz):
            part = part + rz[d - 1, rows]
        for i in range(high - low):
            place = low + i
            s2z[place, 0:H_Z, :] = part[i * H_Z:(i + 1) * H_Z]
            d = rel_z[place]
            if d:
                push(s2z.at[place], rz2.at[d - 1], RS_Z2, y_id(d))

    sum_group(0)
    sum_group_z(0)
    sum_group(1)
    sum_group_z(1)
    sum_group(2)

    sum_z = s2z[ny - 1]
    received(rz2, RS_Z2)
    for d in range(1, ny):
        sum_z = sum_z + rz2[d - 1]
    sum_y = s2y[nz - 1, 0:H_Y]
    received(ry2.at[:, pl.ds(0, H_Y)], RS_Y2)
    for d in range(1, nz):
        sum_y = sum_y + ry2[d - 1, 0:H_Y]
    grad_v[0:H_Y, :] = sum_y
    grad_v[H_Y:16, :] = sum_z[0:H_Z - 1]
    gradient = grad_v[...]
    scaled = gradient / sum_z[H_Z - 1:H_Z]

    first_own = y * nz
    own = first_own + nz - 1
    dirs[own] = scaled.astype(BF16)
    cuts = list(zip(AG_CUTS, AG_CUTS[1:] + (nz,)))
    for d in far_first(nz):
        place = place_of(nz - d, nz)
        group = max(g for g, (low, high) in enumerate(cuts) if low <= place)
        push(dirs.at[own], dirs.at[first_own + place], AG_1, z_id(d), group)
    sent(rz, RS_Z)
    sent(ry.at[:, pl.ds(0, nz * H_Y)], RS_Y)
    sent(rz2, RS_Z2)
    sent(ry2.at[:, pl.ds(0, H_Y)], RS_Y2)
    for g, (low, high) in reversed(list(enumerate(cuts))):
        received(dirs.at[pl.ds(first_own + low, min(high, nz - 1) - low)], AG_1, g)
        part = pl.ds(first_own + low, high - low)
        for d in far_first(ny):
            push(dirs.at[part], dirs.at[part], AG_2, y_id(d))
    place_copy.wait()
    sent(dirs.at[pl.ds(0, nz - 1)], AG_1)
    received(dirs.at[pl.ds(0, mb - nz)], AG_2)

    def image_of(first):
        def one(j, carry):
            r = first + j
            picked = []
            for k in range(slots):
                picked.append(dirs[place_s[k, r]])
            left = jnp.concatenate(picked, axis=1)
            right = jnp.concatenate([a_v[r, k] for k in range(slots)], axis=1)
            out = lax.dot_general(left, right, (((1,), (1,)), ((), ())), preferred_element_type=F32)
            img_f[r] = out
            img_b[r] = out.astype(BF16)
            return carry

        lax.fori_loop(0, rb_own, one, 0, unroll=True)

    for i in range(nmp - 1):
        first = mp_of[i] * rb_own
        image_of(first)
        push(img_b.at[pl.ds(first, rb_own)], ri.at[i], RS_I, mp_id(i))
    mine = pl.ds(mp * rb_own, rb_own)
    image_of(mp * rb_own)
    total = img_f[mine]
    received(ri, RS_I)
    for i in range(nmp - 1):
        total = total + ri[i].astype(F32)
    img[mine] = total

    squares = jnp.concatenate(
        [jnp.sum(total * total, axis=0), gradient * scaled, jnp.zeros((96, 128), F32)], axis=0)
    nsrc[0] = jnp.sum(squares.T, axis=0, keepdims=True)
    for i in range(2 * nz - 1):
        push(nsrc.at[0], n1_r.at[i], N_1, zc_id(i))
    for i in range(nmp - 1):
        push(img.at[mine], img.at[mine], AG_I, mp_id(i))
    sent(dirs.at[pl.ds(0, mb - nz)], AG_2)
    sent(ri, RS_I)
    received(n1_r, N_1)
    acc = nsrc[0]
    for i in range(nz - 1):
        acc = acc + n1_r[i]
    other = n1_r[nz - 1]
    for i in range(nz, 2 * nz - 1):
        other = other + n1_r[i]
    own_x = pl.ds(x * ny, 1)
    n2_r[own_x] = (acc + other)[None]
    for i in range(1, nx * ny):
        push(n2_r.at[own_x], n2_r.at[pl.ds(x * ny + i % ny, 1)], N_2, yx_id(i))
    sent(n1_r, N_1)
    received(img.at[pl.ds(0, rb - rb_own)], AG_I)
    out_copy = pltpu.make_async_copy(img, img_hbm, out_sem)
    out_copy.start()
    sent(img.at[pl.ds(0, rb - rb_own)], AG_I)
    received(n2_r.at[pl.ds(0, nx * ny - 1)], N_2)
    acc = n2_r[0]
    for i in range(1, nx * ny):
        acc = acc + n2_r[i]
    wide = jnp.broadcast_to(acc, (16, 128))
    sub = lax.broadcasted_iota(jnp.int32, (16, 128), 0)
    lane16 = lax.broadcasted_iota(jnp.int32, (16, 128), 1)
    image_norm = jnp.sum(jnp.where(lane16 == sub, wide, 0.0), axis=1, keepdims=True)
    grad_norm = jnp.sum(jnp.where(lane16 == sub + 16, wide, 0.0), axis=1, keepdims=True)
    step = grad_norm / (image_norm + eps)
    small_ref[0] = scaled
    small_ref[1] = jnp.broadcast_to(step, (16, 128))
    out_copy.wait()
    sent(n2_r.at[pl.ds(0, nx * ny - 1)], N_2)


def update(small_ref, img_ref, it_ref, res_ref, itn_ref, resn_ref):
    step = small_ref[1]
    itn_ref[0, 0] = it_ref[0, 0] + step * small_ref[0]
    resn_ref[...] = res_ref[...] - step[None] * img_ref[...]


def local(ray_matrix, block_cols, iterate, residual):
    nmp = lax.axis_size("mp")
    nz = lax.axis_size("ray") // NY
    rb, slots = block_cols.shape
    mb = nz * NY
    rb_own = rb // nmp
    vmem = lambda *shape: pltpu.VMEM(shape, F32)
    dma = lambda n: pltpu.SemaphoreType.DMA((n,))
    scratch = [
        pltpu.VMEM(ray_matrix.shape, BF16),
        pltpu.VMEM(residual.shape, F32),
        pltpu.VMEM((slots, rb), jnp.int32),
        pltpu.VMEM((slots, rb), jnp.int32),
        pltpu.SMEM((slots, rb), jnp.int32),
        vmem(24 * rb * slots, 128),
        vmem(NY * PAD * H_Y, 128),
        vmem(mb * H_Z, 128),
        vmem(NY - 1, PAD * H_Y, 128),
        vmem(nz - 1, NY * H_Z, 128),
        vmem(nz, 16, 128),
        vmem(NY, 8, 128),
        vmem(nz - 1, 16, 128),
        vmem(NY - 1, 8, 128),
        vmem(16, 128),
        pltpu.VMEM((mb, 16, 128), BF16),
        vmem(rb, 16, 128),
        pltpu.VMEM((rb, 16, 128), BF16),
        pltpu.VMEM((nmp - 1, rb_own, 16, 128), BF16),
        vmem(rb, 16, 128),
        vmem(1, 1, 128),
        vmem(2 * nz - 1, 1, 128),
        vmem(nmp // 2 * NY, 1, 128),
        dma(CHUNKS), *[pltpu.SemaphoreType.DMA] * 4,
    ]
    scratch += [dma(PHASES), dma(PHASES)]
    any_spec = pl.BlockSpec(memory_space=pl.ANY)
    small, img = pl.pallas_call(
        functools.partial(kernel, nz, nmp),
        out_shape=(
            jax.ShapeDtypeStruct((2, 16, 128), F32),
            jax.ShapeDtypeStruct(residual.shape, F32),
        ),
        in_specs=[any_spec] * 3,
        out_specs=(pl.BlockSpec(memory_space=pltpu.VMEM), any_spec),
        scratch_shapes=scratch,
        compiler_params=pltpu.CompilerParams(
            collective_id=0, has_side_effects=True, vmem_limit_bytes=61 * 2**20),
        cost_estimate=pl.CostEstimate(flops=300_000_000, bytes_accessed=5_000_000, transcendentals=0),
        name="cgls",
    )(ray_matrix, block_cols.T, residual)
    return pl.pallas_call(
        update,
        out_shape=(
            jax.ShapeDtypeStruct(iterate.shape, F32),
            jax.ShapeDtypeStruct(residual.shape, F32),
        ),
        in_specs=[pl.BlockSpec(memory_space=pltpu.VMEM)] * 4,
        out_specs=(pl.BlockSpec(memory_space=pltpu.VMEM),) * 2,
        compiler_params=pltpu.CompilerParams(vmem_limit_bytes=61 * 2**20),
        cost_estimate=pl.CostEstimate(flops=200_000, bytes_accessed=800_000, transcendentals=0),
        name="update",
    )(small, img, iterate, residual)


def solution(mesh):
    in_specs = (
        P("ray", "mp", None, None),
        P("ray", "mp"),
        P("mp", "ray", None, None),
        P("ray", None, None),
    )
    out_specs = (P("mp", "ray", None, None), P("ray", None, None))
    return jax.shard_map(local, mesh=mesh, in_specs=in_specs, out_specs=out_specs, check_vma=False)
```

```python
import functools
import jax
import jax.numpy as jnp
from jax import lax
from jax.experimental import pallas as pl
from jax.experimental.pallas import tpu as pltpu
from jax.sharding import PartitionSpec as P

MESH = pl.DeviceIdType.MESH
F32 = jnp.float32
BF16 = jnp.bfloat16
eps = 1e-06

NY = 8
H_Y = 11
H_Z = 6
CHUNKS = 8
RS_CUTS = (0, 4, 9)
STRIDE = 8
RZ_CUTS = (0, 4)
AG_CUTS = (0, 3, 7)

RS_Z, RS_Y, RS_Z2, RS_Y2, AG_1, AG_2, RS_I, AG_I, N_1, N_2, PHASES = 0, 2, 5, 6, 7, 10, 11, 12, 13, 14, 15
PAD = STRIDE * len(RS_CUTS)


def far_first(n):
    return sorted(range(1, n), key=lambda d: -min(d, n - d))


def place_of(rel, n):
    return n - 1 - 2 * rel if rel < n // 2 else 2 * rel - n


def kernel(nz, nmp, a_hbm, cols_hbm, res_hbm, small_ref, img_hbm,
           a_v, res_v, cols_v, place_v, place_s, terms, gy, gz, ry, rz, s2y, s2z, ry2, rz2, grad_v,
           dirs, img_f, img_b, ri, img, nsrc, n1_r, n2_r,
           a_sem, res_sem, cv_sem, ps_sem, out_sem,
           send_sem, recv_sem):
    ny = NY
    mb = nz * ny
    rb = a_v.shape[0]
    rb_own = rb // nmp
    per = rb // CHUNKS
    me = lax.axis_index("ray")
    mp = lax.axis_index("mp")
    z = me // ny
    y = me % ny
    y_of = [None] + [(y + d) % ny for d in range(1, ny)]
    z_of = [None] + [(z + d) % nz for d in range(1, nz)]
    y_id = lambda d: (z * ny + y_of[d], mp)
    z_id = lambda d: (z_of[d] * ny + y, mp)

    nx = nmp // 2
    x = mp // 2
    core = mp % 2
    other_core = x * 2 + 1 - core
    mp_of = [((x + d) % nx) * 2 + c for d in far_first(nx) for c in (core, 1 - core)] + [other_core]
    mp_id = lambda i: (me, mp_of[i])

    def zc_id(i):
        if i < nz - 1:
            return z_id(i + 1)
        d = i - (nz - 1)
        return (((z + d) % nz) * ny + y, other_core)

    def yx_id(i):
        return (z * ny + (y + i % ny) % ny, ((x + i // ny) % nx) * 2 + core)

    cv_copy = pltpu.make_async_copy(cols_hbm, cols_v, cv_sem)
    cv_copy.start()
    res_copy = pltpu.make_async_copy(res_hbm, res_v, res_sem)
    res_copy.start()
    a_copies = []
    for i in range(CHUNKS):
        part = pl.ds(i * per, per)
        copy = pltpu.make_async_copy(a_hbm.at[part], a_v.at[part], a_sem.at[i])
        copy.start()
        a_copies.append(copy)

    barrier = pltpu.get_barrier_semaphore()
    for d in far_first(nz):
        pl.semaphore_signal(barrier, inc=1, device_id=z_id(d), device_id_type=MESH)
    for d in far_first(ny):
        pl.semaphore_signal(barrier, inc=1, device_id=y_id(d), device_id_type=MESH)
    for d in range(nmp - 1):
        pl.semaphore_signal(barrier, inc=1, device_id=mp_id(d), device_id_type=MESH)
    for i in range(nz, 2 * nz - 1):
        pl.semaphore_signal(barrier, inc=1, device_id=zc_id(i), device_id_type=MESH)
    for i in range(ny, nx * ny):
        if i % ny:
            pl.semaphore_signal(barrier, inc=1, device_id=yx_id(i), device_id_type=MESH)
    greeted = (nz - 1) + (ny - 1) + (nmp - 1) + (nz - 1) + (nx - 1) * (ny - 1)

    def push(src, dst, phase, target, group=0):
        pltpu.make_async_remote_copy(
            src_ref=src, dst_ref=dst, send_sem=send_sem.at[phase], recv_sem=recv_sem.at[phase + group],
            device_id=target, device_id_type=MESH).start()

    def all_of(ref, phase, group=0):
        return pltpu.make_async_remote_copy(
            src_ref=ref, dst_ref=ref, send_sem=send_sem.at[phase], recv_sem=recv_sem.at[phase + group],
            device_id=y_id(1), device_id_type=MESH)

    def received(ref, phase, group=0):
        all_of(ref, phase, group).wait_recv()

    def sent(ref, phase):
        all_of(ref, phase).wait_send()

    slots = cols_v.shape[0]

    def one_hot(blocks, place):
        block = lax.broadcasted_iota(jnp.int32, (blocks, rb), 0)
        parts = [(place(cols_v[k:k + 1, :]) == block).astype(F32) for k in range(slots)]
        hot = jnp.concatenate(parts, axis=1).astype(BF16)
        return jnp.concatenate([hot, hot, hot], axis=1)

    cv_copy.wait()

    def near(c, mine, n):
        rel = c - mine
        rel = jnp.where(rel < 0, rel + n, rel)
        return jnp.where(rel < n // 2, n - 1 - 2 * rel, 2 * rel - n)

    near_z = lambda c: near(c // ny, z, nz)

    def spot(place):
        return place + sum(
            jnp.where(place >= low, STRIDE - low + last, 0) for last, low in zip(RS_CUTS, RS_CUTS[1:]))

    hot_z = one_hot(mb, lambda c: (c // ny) * ny + near(c % ny, y, ny))
    hot_y = one_hot(ny * PAD, lambda c: (c % ny) * PAD + spot(near_z(c)))
    place_v[...] = (cols_v[...] % ny) * nz + near_z(cols_v[...])
    place_copy = pltpu.make_async_copy(place_v, place_s, ps_sem)
    place_copy.start()

    tiles = rb * slots
    res_copy.wait()
    ones = jnp.ones((16, 128), BF16)
    for i in range(CHUNKS):
        a_copies[i].wait()

        def products(j, carry):
            r = i * per + j
            left = jnp.concatenate([res_v[r].astype(BF16), ones], axis=0)
            right = jnp.concatenate([a_v[r, k] for k in range(slots)], axis=1)
            out = jnp.dot(left, right, preferred_element_type=F32)
            for k in range(slots):
                terms[pl.ds(k * rb + r, 24, stride=tiles), :] = out[:24, k * 128:(k + 1) * 128]
            return carry

        lax.fori_loop(0, per, products, 0, unroll=True)

    def split(h):
        t = terms[pl.ds(h * tiles, tiles), :]
        hi = t.astype(BF16)
        rest = t - hi.astype(F32)
        mid = rest.astype(BF16)
        low = (rest - mid.astype(F32)).astype(BF16)
        return jnp.concatenate([hi, mid, low], axis=0)

    def segment(hot, dst, rows, first):
        for h in range(0, rows, 2):
            n = min(2, rows - h)
            right = jnp.concatenate([split(first + h + i) for i in range(n)], axis=1)
            out = jnp.dot(hot, right, preferred_element_type=F32)
            for i in range(n):
                dst[pl.ds(h + i, hot.shape[0], stride=rows), :] = out[:, i * 128:(i + 1) * 128]

    segment(hot_y, gy, H_Y, 0)
    pl.semaphore_wait(barrier, greeted)
    len_z = ny * H_Z
    len_y = PAD * H_Y
    groups = list(zip(RS_CUTS, RS_CUTS[1:] + (nz,)))
    rows_of = lambda g: pl.ds(g * STRIDE * H_Y, (groups[g][1] - groups[g][0]) * H_Y)
    groups_z = list(zip(RZ_CUTS, RZ_CUTS[1:] + (ny,)))
    rows_z = lambda g: pl.ds(groups_z[g][0] * H_Z, (groups_z[g][1] - groups_z[g][0]) * H_Z)
    for g in range(len(groups)):
        rows = rows_of(g)
        for d in far_first(ny):
            push(gy.at[pl.ds(y_of[d] * len_y + rows.start, rows.size)], ry.at[d - 1, rows], RS_Y, y_id(d), g)
    segment(hot_z, gz, H_Z, H_Y)
    for g in range(len(groups_z)):
        rows = rows_z(g)
        for d in far_first(nz):
            push(gz.at[pl.ds(z_of[d] * len_z + rows.start, rows.size)], rz.at[d - 1, rows], RS_Z, z_id(d), g)
    rel_of = {place_of(rel, nz): rel for rel in range(nz)}

    def sum_group(g):
        low, high = groups[g]
        rows = rows_of(g)
        part = gy[pl.ds(pl.multiple_of(y * len_y + rows.start, 8), rows.size), :]
        received(ry.at[:, rows], RS_Y, g)
        for d in range(1, ny):
            part = part + ry[d - 1, rows]
        for i in range(high - low):
            place = low + i
            s2y[place, 0:H_Y, :] = part[i * H_Y:(i + 1) * H_Y]
            d = rel_of[place]
            if d:
                push(s2y.at[place, pl.ds(0, H_Y)], ry2.at[d - 1, pl.ds(0, H_Y)], RS_Y2, z_id(d))

    rel_z = {place_of(rel, ny): rel for rel in range(ny)}

    def sum_group_z(g):
        low, high = groups_z[g]
        rows = rows_z(g)
        part = gz[pl.ds(pl.multiple_of(z * len_z + rows.start, 8), rows.size), :]
        received(rz.at[:, rows], RS_Z, g)
        for d in range(1, nz):
            part = part + rz[d - 1, rows]
        for i in range(high - low):
            place = low + i
            s2z[place, 0:H_Z, :] = part[i * H_Z:(i + 1) * H_Z]
            d = rel_z[place]
            if d:
                push(s2z.at[place], rz2.at[d - 1], RS_Z2, y_id(d))

    sum_group(0)
    sum_group_z(0)
    sum_group(1)
    sum_group_z(1)
    sum_group(2)

    sum_z = s2z[ny - 1]
    received(rz2, RS_Z2)
    for d in range(1, ny):
        sum_z = sum_z + rz2[d - 1]
    sum_y = s2y[nz - 1, 0:H_Y]
    received(ry2.at[:, pl.ds(0, H_Y)], RS_Y2)
    for d in range(1, nz):
        sum_y = sum_y + ry2[d - 1, 0:H_Y]
    grad_v[0:H_Y, :] = sum_y
    grad_v[H_Y:16, :] = sum_z[0:H_Z - 1]
    gradient = grad_v[0:16, :]
    scaled = gradient / sum_z[H_Z - 1:H_Z]

    first_own = y * nz
    own = first_own + nz - 1
    dirs[own] = scaled.astype(BF16)
    cuts = list(zip(AG_CUTS, AG_CUTS[1:] + (nz,)))
    for d in far_first(nz):
        place = place_of(nz - d, nz)
        group = max(g for g, (low, high) in enumerate(cuts) if low <= place)
        push(dirs.at[own], dirs.at[first_own + place], AG_1, z_id(d), group)
    sent(rz, RS_Z)
    sent(ry.at[:, pl.ds(0, nz * H_Y)], RS_Y)
    sent(rz2, RS_Z2)
    sent(ry2.at[:, pl.ds(0, H_Y)], RS_Y2)
    for g, (low, high) in reversed(list(enumerate(cuts))):
        received(dirs.at[pl.ds(first_own + low, min(high, nz - 1) - low)], AG_1, g)
        part = pl.ds(first_own + low, high - low)
        for d in far_first(ny):
            push(dirs.at[part], dirs.at[part], AG_2, y_id(d))
    place_copy.wait()
    sent(dirs.at[pl.ds(0, nz - 1)], AG_1)
    received(dirs.at[pl.ds(0, mb - nz)], AG_2)

    def image_of(first):
        def one(j, carry):
            r = first + j
            picked = []
            for k in range(slots):
                picked.append(dirs[place_s[k, r]])
            left = jnp.concatenate(picked, axis=1)
            right = jnp.concatenate([a_v[r, k] for k in range(slots)], axis=1)
            out = lax.dot_general(left, right, (((1,), (1,)), ((), ())), preferred_element_type=F32)
            img_f[r] = out
            img_b[r] = out.astype(BF16)
            return carry

        lax.fori_loop(0, rb_own, one, 0, unroll=True)

    for i in range(nmp - 1):
        first = mp_of[i] * rb_own
        image_of(first)
        push(img_b.at[pl.ds(first, rb_own)], ri.at[i], RS_I, mp_id(i))
    mine = pl.ds(mp * rb_own, rb_own)
    image_of(mp * rb_own)
    total = img_f[mine]
    received(ri, RS_I)
    for i in range(nmp - 1):
        total = total + ri[i].astype(F32)
    img[mine] = total

    squares = jnp.concatenate(
        [jnp.sum(total * total, axis=0), gradient * scaled, jnp.zeros((96, 128), F32)], axis=0)
    nsrc[0] = jnp.sum(squares.T, axis=0, keepdims=True)
    for i in range(2 * nz - 1):
        push(nsrc.at[0], n1_r.at[i], N_1, zc_id(i))
    for i in range(nmp - 1):
        push(img.at[mine], img.at[mine], AG_I, mp_id(i))
    sent(dirs.at[pl.ds(0, mb - nz)], AG_2)
    sent(ri, RS_I)
    received(n1_r, N_1)
    acc = nsrc[0]
    for i in range(nz - 1):
        acc = acc + n1_r[i]
    other = n1_r[nz - 1]
    for i in range(nz, 2 * nz - 1):
        other = other + n1_r[i]
    own_x = pl.ds(x * ny, 1)
    n2_r[own_x] = (acc + other)[None]
    for i in range(1, nx * ny):
        push(n2_r.at[own_x], n2_r.at[pl.ds(x * ny + i % ny, 1)], N_2, yx_id(i))
    sent(n1_r, N_1)
    received(img.at[pl.ds(0, rb - rb_own)], AG_I)
    out_copy = pltpu.make_async_copy(img, img_hbm, out_sem)
    out_copy.start()
    sent(img.at[pl.ds(0, rb - rb_own)], AG_I)
    received(n2_r.at[pl.ds(0, nx * ny - 1)], N_2)
    acc = n2_r[0]
    for i in range(1, nx * ny):
        acc = acc + n2_r[i]
    wide = jnp.broadcast_to(acc, (16, 128))
    sub = lax.broadcasted_iota(jnp.int32, (16, 128), 0)
    lane16 = lax.broadcasted_iota(jnp.int32, (16, 128), 1)
    image_norm = jnp.sum(jnp.where(lane16 == sub, wide, 0.0), axis=1, keepdims=True)
    grad_norm = jnp.sum(jnp.where(lane16 == sub + 16, wide, 0.0), axis=1, keepdims=True)
    step = grad_norm / (image_norm + eps)
    small_ref[0] = scaled
    small_ref[1] = jnp.broadcast_to(step, (16, 128))
    out_copy.wait()
    sent(n2_r.at[pl.ds(0, nx * ny - 1)], N_2)


def update(small_ref, img_ref, it_ref, res_ref, itn_ref, resn_ref):
    step = small_ref[1]
    itn_ref[0, 0] = it_ref[0, 0] + step * small_ref[0]
    resn_ref[...] = res_ref[...] - step[None] * img_ref[...]


def local(ray_matrix, block_cols, iterate, residual):
    nmp = lax.axis_size("mp")
    nz = lax.axis_size("ray") // NY
    rb, slots = block_cols.shape
    mb = nz * NY
    rb_own = rb // nmp
    vmem = lambda *shape: pltpu.VMEM(shape, F32)
    dma = lambda n: pltpu.SemaphoreType.DMA((n,))
    scratch = [
        pltpu.VMEM(ray_matrix.shape, BF16),
        pltpu.VMEM(residual.shape, F32),
        pltpu.VMEM((slots, rb), jnp.int32),
        pltpu.VMEM((slots, rb), jnp.int32),
        pltpu.SMEM((slots, rb), jnp.int32),
        vmem(25 * rb * slots, 128),
        vmem(NY * PAD * H_Y + 16, 128),
        vmem(mb * H_Z + 16, 128),
        vmem(NY - 1, PAD * H_Y, 128),
        vmem(nz - 1, NY * H_Z, 128),
        vmem(nz, 16, 128),
        vmem(NY, 8, 128),
        vmem(nz - 1, 16, 128),
        vmem(NY - 1, 8, 128),
        vmem(24, 128),
        pltpu.VMEM((mb, 16, 128), BF16),
        vmem(rb, 16, 128),
        pltpu.VMEM((rb, 16, 128), BF16),
        pltpu.VMEM((nmp - 1, rb_own, 16, 128), BF16),
        vmem(rb, 16, 128),
        vmem(1, 1, 128),
        vmem(2 * nz - 1, 1, 128),
        vmem(nmp // 2 * NY, 1, 128),
        dma(CHUNKS), *[pltpu.SemaphoreType.DMA] * 4,
    ]
    scratch += [dma(PHASES), dma(PHASES)]
    any_spec = pl.BlockSpec(memory_space=pl.ANY)
    small, img = pl.pallas_call(
        functools.partial(kernel, nz, nmp),
        out_shape=(
            jax.ShapeDtypeStruct((2, 16, 128), F32),
            jax.ShapeDtypeStruct(residual.shape, F32),
        ),
        in_specs=[any_spec] * 3,
        out_specs=(pl.BlockSpec(memory_space=pltpu.VMEM), any_spec),
        scratch_shapes=scratch,
        compiler_params=pltpu.CompilerParams(
            collective_id=0, has_side_effects=True, vmem_limit_bytes=61 * 2**20),
        cost_estimate=pl.CostEstimate(flops=300_000_000, bytes_accessed=5_000_000, transcendentals=0),
        name="cgls",
    )(ray_matrix, block_cols.T, residual)
    return pl.pallas_call(
        update,
        out_shape=(
            jax.ShapeDtypeStruct(iterate.shape, F32),
            jax.ShapeDtypeStruct(residual.shape, F32),
        ),
        in_specs=[pl.BlockSpec(memory_space=pltpu.VMEM)] * 4,
        out_specs=(pl.BlockSpec(memory_space=pltpu.VMEM),) * 2,
        compiler_params=pltpu.CompilerParams(vmem_limit_bytes=61 * 2**20),
        cost_estimate=pl.CostEstimate(flops=200_000, bytes_accessed=800_000, transcendentals=0),
        name="update",
    )(small, img, iterate, residual)


def solution(mesh):
    in_specs = (
        P("ray", "mp", None, None),
        P("ray", "mp"),
        P("mp", "ray", None, None),
        P("ray", None, None),
    )
    out_specs = (P("mp", "ray", None, None), P("ray", None, None))
    return jax.shard_map(local, mesh=mesh, in_specs=in_specs, out_specs=out_specs, check_vma=False)
```
